256 devices in a mesh: dp: 64 (over z, x, core), feat: 4 (over y).
Axes of the slice: x: 4, y: 4, z: 8, core: 2. Of those that a mesh axis runs over, the one named last changes fastest.
Arguments:
- table: int32 [65536, 2048], P('dp', 'feat'), may hold values from 0 to 63
- sample_rows: int32 [32768], P('dp'), may hold values from 0 to 1023
- gradients: bfloat16 [32768, 16], P('dp'), may hold values from -6 to 6
- hessian: bfloat16 [32768], P('dp'), may hold values from 0.0049743652 to 0.049804688
- node_ids: int32 [32768], P('dp'), may hold values from 0 to 1
- split_feature: int32 [2], replicated, may hold values from 0 to 2047
- split_bin: int32 [2], replicated, may hold values from 0 to 63
Outputs:
- best_gain: float32 [2, 2048], P(None, 'feat')
- leaf_values: float32 [4, 16], replicated
The draws below stay inside these ranges and needn't reach their ends.
Inputs may be any that keep to these rules, and one draw needn't show every extreme that they name: `sample_rows`: each entry names a row of the same device's block of 1024 table rows.
All inputs are finite; a program needn't handle non-finite values.
Results may differ from the reference program's by a relative error of at most 0.0003.
Values sent between devices are 32-bit elements; how exact they have to be, the bound alone decides.
A program may use at most 64 MiB of HBM per device.

```python
import math
import jax
import jax.numpy as jnp
import numpy as np
from jax import lax

F = 2048
BINS = 64
K = 16
NODES = 2
S_DEV = 512
TAB_DEV = 1024
SAMPLES = 32768
TAB_ROWS = 65536


def set_ends(array, key, low, largest):
    shape = array.shape
    place = [jax.random.randint(jax.random.fold_in(key, axis), (), 0, shape[axis]) for axis in range(len(shape))]
    array = array.at[tuple(place)].set(low)
    longest = shape.index(max(shape))
    place[longest] = (place[longest] + 1) % shape[longest]
    return array.at[tuple(place)].set(largest)


def levels(stream_key, shape, split, low, largest):
    loudness, own = 1.0, jax.random.fold_in(stream_key, 6)
    for position, shards_of in split:
        heights = jnp.exp(jax.random.uniform(jax.random.fold_in(own, position), (shards_of,), jnp.float32, low / len(split), largest / len(split)))
        loudness = loudness * jnp.repeat(heights, shape[position] // shards_of).reshape([-1 if axis == position else 1 for axis in range(len(shape))])
    return loudness


def rank_table(amount, skew):
    portions = [(1 << 20) // math.isqrt(standing ** skew) + 1 for standing in range(1, amount + 1)]
    width = 1 + sum(portions) // (1 << 30)
    return np.cumsum(np.array([max(1, weight // width) for weight in portions]))


def skewed_ids(stream_key, extent, amount, slope):
    listing = rank_table(amount, slope)
    pick = jax.random.randint(jax.random.fold_in(stream_key, 1), extent, 0, int(listing[amount - 1]))
    grade = jnp.searchsorted(jnp.asarray(listing, jnp.int32), pick, side="right")
    return jax.random.permutation(jax.random.fold_in(stream_key, 2), amount)[grade].astype(jnp.int32)


def normal_values(rng, shape, width, limit, cuts=(), held_as=jnp.bfloat16):
    loudness = levels(rng, shape, cuts, -0.22, 0.18) if cuts else 1.0
    array = jax.random.normal(rng, shape, jnp.float32) * width * loudness
    return jnp.minimum(jnp.maximum(array, -limit), limit).astype(held_as)


def setup_inputs(seed: int = 0) -> dict:
    streams_of = jax.random.split(jax.random.key(seed), 8)
    table = set_ends(jax.random.randint(streams_of[0], (TAB_ROWS, F), 0, BINS), jax.random.fold_in(streams_of[0], 1), 0, BINS - 1).astype(jnp.int32)
    sample_rows = set_ends(jax.random.randint(streams_of[1], (SAMPLES,), 0, TAB_DEV), jax.random.fold_in(streams_of[1], 1), 0, TAB_DEV - 1).astype(jnp.int32)
    gradients = normal_values(streams_of[2], (SAMPLES, K), 1.0, 6.0, ((0, 64),))
    hessian = jnp.clip(jnp.exp(math.log(0.049804688) - 2.3038113 * jax.random.uniform(streams_of[3], (SAMPLES,), jnp.float32) ** levels(streams_of[3], (SAMPLES,), ((0, 64),), -0.2, 0.2)), 0.0049743652, 0.049804688).astype(jnp.bfloat16)
    node_ids = set_ends(skewed_ids(streams_of[4], (SAMPLES,), NODES, 2), jax.random.fold_in(streams_of[4], 3), 0, NODES - 1).astype(jnp.int32)
    split_feature = jax.random.randint(streams_of[5], (NODES,), 0, F).astype(jnp.int32)
    split_bin = jax.random.randint(streams_of[6], (NODES,), 0, BINS).astype(jnp.int32)
    return dict(table=table, sample_rows=sample_rows, gradients=gradients, hessian=hessian, node_ids=node_ids, split_feature=split_feature, split_bin=split_bin)


LAMBDA_REG = 1.0
GAIN_WEIGHT = 0.01


def split_gain(left, total):
    grad_left = left[..., :K]
    hess_left = left[..., K]
    grad_total = total[..., :K]
    hess_total = total[..., K]
    grad_right = grad_total - grad_left
    hess_right = hess_total - hess_left
    score = jnp.sum(grad_left * grad_left, axis=-1) / (hess_left + LAMBDA_REG)
    score = score + jnp.sum(grad_right * grad_right, axis=-1) / (hess_right + LAMBDA_REG)
    score = score - jnp.sum(grad_total * grad_total, axis=-1) / (hess_total + LAMBDA_REG)
    return score * (GAIN_WEIGHT / K)


def reference(table, sample_rows, gradients, hessian, node_ids, split_feature, split_bin):
    block = jnp.arange(SAMPLES, dtype=jnp.int32) // S_DEV
    global_rows = (block * TAB_DEV + sample_rows).astype(jnp.int32)
    picked = jnp.take(table, global_rows, axis=0)
    channels = jnp.concatenate([gradients, hessian[:, None]], axis=1).astype(jnp.float32)

    def per_feature(column):
        return jax.ops.segment_sum(channels, node_ids * BINS + column, num_segments=NODES * BINS)

    hist = lax.map(per_feature, picked.T)
    hist = hist.reshape(F, NODES, BINS, K + 1)
    left = jnp.cumsum(hist, axis=2)
    total = left[:, :, -1:, :]
    best_gain = jnp.max(split_gain(left, total), axis=2).T
    left_pick = left[split_feature, jnp.arange(NODES), split_bin]
    total_pick = total[0, :, 0, :]
    left_value = -left_pick[:, :K] / (left_pick[:, K:] + LAMBDA_REG)
    right_value = -(total_pick[:, :K] - left_pick[:, :K]) / (total_pick[:, K:] - left_pick[:, K:] + LAMBDA_REG)
    leaf_values = jnp.stack([left_value, right_value], axis=1).reshape(2 * NODES, K)
    return best_gain, leaf_values
```

```python
import functools

import jax
import jax.numpy as jnp
from jax import lax
from jax.experimental import pallas as pl
from jax.experimental.pallas import tpu as pltpu
from jax.sharding import PartitionSpec as P

BINS = 64
K = 16
NODES = 2
LAMBDA_REG = 1.0
GAIN_WEIGHT = 0.01

NX = 8
NZ = 8
NY = 4
S = 512
TAB = 1024
WIDTH = 512
OWN = 8
ROWS = 40
LANES = OWN * BINS
AHEAD = 3
MESH = pl.DeviceIdType.MESH
F32 = jnp.float32
BF16 = jnp.bfloat16


def iota(shape, dim):
    return lax.broadcasted_iota(jnp.int32, shape, dim)


def kernel(
    sf_ref, sb_ref, table_ref, rows_ref, grad_ref, hess_ref, node_ref,
    best_ref, leaf_ref,
    tab, pk, rx, blob, wt, acc, rz, ysend, yrecv, g1, g1r, g2, g2r,
    tab_sem, rx_send, rx_recv, ch_send, ch_recv, rz_send, rz_recv, y_send, y_recv, g_send, g_recv,
):
    d = lax.axis_index("dp")
    y = lax.axis_index("feat")
    z = d // NX
    xd = d % NX

    def xpeer(r):
        return (z * NX + lax.rem(xd + r, NX), y)

    def zpeer(q):
        return (lax.rem(z + q + NZ, NZ) * NX + xd, y)

    def ypeer(r):
        return (d, lax.rem(y + r, NY))

    load = pltpu.make_async_copy(table_ref, tab, tab_sem)
    load.start()

    barrier = pltpu.get_barrier_semaphore()
    for r in range(1, NX):
        pl.semaphore_signal(barrier, inc=1, device_id=xpeer(r), device_id_type=MESH)
    for r in range(1, NZ):
        pl.semaphore_signal(barrier, inc=1, device_id=zpeer(r), device_id_type=MESH)
    for r in range(1, NY):
        pl.semaphore_signal(barrier, inc=1, device_id=ypeer(r), device_id_type=MESH)

    grad_t = grad_ref[...].astype(F32)
    hess = hess_ref[...].astype(F32)
    node = node_ref[...].astype(F32)
    for j in range(S // 128):
        lanes = slice(j * 128, (j + 1) * 128)
        blob[0, j * K:(j + 1) * K, :] = grad_t[:, lanes]
        blob[0, 64 + 2 * j:65 + 2 * j, :] = hess[:, lanes]
        blob[0, 65 + 2 * j:66 + 2 * j, :] = node[:, lanes]

    pl.semaphore_wait(barrier, NX + NZ + NY - 3)

    sib = lax.rem(xd, 2)
    sib_rel = 1 - 2 * sib

    def sibling():
        return (z * NX + xd + sib_rel, y)

    def ch_copy(src_slot, dst_slot, where, k):
        return pltpu.make_async_remote_copy(
            src_ref=blob.at[src_slot], dst_ref=blob.at[dst_slot],
            send_sem=ch_send.at[k], recv_sem=ch_recv.at[dst_slot],
            device_id=where, device_id_type=MESH,
        )

    first = [ch_copy(0, 4 - m, xpeer(2 * m), m) for m in range(1, 4)] + [ch_copy(0, 4, sibling(), 0)]
    for c in first:
        c.start()

    hot = jnp.where(iota((TAB, S), 0) == rows_ref[...], 1.0, 0.0).astype(BF16)
    load.wait()
    for j in range(WIDTH // 128):
        part = tab[:, j * 128:(j + 1) * 128].astype(F32).astype(BF16)
        pk[j * 128:(j + 1) * 128, :] = lax.dot_general(
            part, hot, (((0,), (0,)), ((), ())), preferred_element_type=F32)

    def chunk_z(i):
        half = (i + 1) // 2
        away = jnp.where(i % 2 == 1, 4 - half, 4 + half)
        away = jnp.where(i == 7, 0, away)
        return lax.rem(z + away, NZ)

    def x_copy(i, r):
        peer_x = lax.rem(xd + r, NX)
        row = pl.multiple_of(chunk_z(i) * (NX * OWN) + peer_x * OWN, OWN)
        return pltpu.make_async_remote_copy(
            src_ref=pk.at[pl.ds(row, OWN), :], dst_ref=rx.at[i, NX - r - 1],
            send_sem=rx_send.at[i], recv_sem=rx_recv.at[i],
            device_id=(z * NX + peer_x, y), device_id_type=MESH,
        )

    def start_chunk(i):
        for r in range(1, NX):
            x_copy(i, r).start()

    for i in range(AHEAD):
        start_chunk(i)

    for c in first[:3]:
        c.wait_recv()
    second = [ch_copy(m, 4 + m, sibling(), 3 + m) for m in range(1, 4)]
    for c in second:
        c.start()

    def weights(slot, place):
        for j in range(S // 128):
            g = blob[slot, j * K:(j + 1) * K, :]
            h = blob[slot, 64 + 2 * j:65 + 2 * j, :]
            n = blob[slot, 65 + 2 * j:66 + 2 * j, :]
            at0 = n == 0.0
            at1 = n == 1.0
            rest = jnp.where(iota((16, 128), 0) == 0, jnp.where(at0, h, 0.0),
                             jnp.where(iota((16, 128), 0) == 1, jnp.where(at1, h, 0.0), 0.0))
            full = jnp.concatenate(
                [jnp.where(at0, g, 0.0), jnp.where(at1, g, 0.0), rest], axis=0)
            wt[place, :, j * 128:(j + 1) * 128] = full.astype(BF16)

    weights(0, 0)
    for m in range(1, 4):
        weights(m, 2 * m)

    ind = []
    for n in range(NODES):
        col = sf_ref[n] - y * WIDTH
        inside = jnp.where((col >= 0) & (col < WIDTH), 1.0, 0.0).astype(F32)
        row = pk[pl.ds(jnp.clip(col, 0, WIDTH - 1), 1), :]
        ind.append(jnp.where(row <= sb_ref[n].astype(F32), inside, 0.0))
    ind.append(jnp.full((1, S), jnp.where(y == 0, 1.0, 0.0).astype(F32)))
    ind.append(jnp.zeros((13, S), F32))
    ind = jnp.concatenate(ind, axis=0).astype(BF16)
    leaf_part = lax.dot_general(
        ind, wt[0], (((1,), (1,)), ((), ())), preferred_element_type=F32)
    ysend[...] = jnp.concatenate([leaf_part[:8], jnp.zeros((8, 80), F32)], axis=1)

    def y_copy(r):
        return pltpu.make_async_remote_copy(
            src_ref=ysend, dst_ref=yrecv.at[NY - r - 1],
            send_sem=y_send, recv_sem=y_recv, device_id=ypeer(r), device_id_type=MESH,
        )

    for r in range(1, NY):
        y_copy(r).start()

    first[3].wait_recv()
    for c in second:
        c.wait_recv()
    for m in range(4):
        weights(4 + m, lax.rem(2 * m + sib_rel + NX, NX))

    level = iota((BINS, S), 0).astype(F32).astype(BF16)
    one = jnp.ones((), BF16)
    zero = jnp.zeros((), BF16)

    def below(value):
        return jnp.where(jnp.broadcast_to(value.astype(BF16), (BINS, S)) <= level, one, zero)

    def z_copy(i, target):
        slot = jnp.where(i == 0, 1, i + 2)
        return pltpu.make_async_remote_copy(
            src_ref=acc.at[i], dst_ref=rz.at[slot],
            send_sem=rz_send.at[i], recv_sem=rz_recv.at[slot],
            device_id=target, device_id_type=MESH,
        )

    def chunk(i, carry):
        @pl.when(i + AHEAD < NZ)
        def _():
            start_chunk(i + AHEAD)

        pltpu.make_async_copy(rx.at[i], rx.at[i], rx_recv.at[i]).wait()
        mine = chunk_z(i) * (NX * OWN) + xd * OWN
        total = None
        for r in range(NX):
            hots = []
            for f in range(OWN):
                value = pk[pl.ds(mine + f, 1), :] if r == 0 else rx[i, r - 1, f:f + 1, :]
                hots.append(below(value))
            part = lax.dot_general(
                wt[r], jnp.concatenate(hots, axis=0), (((1,), (1,)), ((), ())),
                preferred_element_type=F32)
            total = part if total is None else total + part
        acc[i] = total[:ROWS]

        @pl.when((i != 0) & (i != 2) & (i != 7))
        def _():
            pltpu.make_async_copy(rz.at[i], rz.at[i], rz_recv.at[i]).wait()
            acc[i] = acc[i] + rz[i]

        @pl.when(i < NZ - 1)
        def _():
            up = (i == 0) | (i % 2 == 1)
            z_copy(i, (lax.rem(z + jnp.where(up, 1, NZ - 1), NZ) * NX + xd, y)).start()

        return carry

    lax.fori_loop(0, NZ, chunk, 0)
    for i in (7, 8):
        pltpu.make_async_copy(rz.at[i], rz.at[i], rz_recv.at[i]).wait()
    left = acc[7] + rz[7] + rz[8]

    total = jnp.broadcast_to(left[:, BINS - 1:BINS], (ROWS, LANES))
    right = total - left
    gains = []
    for n in range(NODES):
        def score(part):
            g = part[n * K:(n + 1) * K]
            h = part[32 + n:33 + n]
            return jnp.sum(g * g, axis=0, keepdims=True) / (h + LAMBDA_REG)
        gains.append((score(left) + score(right) - score(total)) * (GAIN_WEIGHT / K))
    gains = jnp.concatenate(gains + [jnp.zeros((6, LANES), F32)], axis=0)

    lane = iota((8, 128), 1)
    row8 = iota((8, 128), 0)
    base = xd * OWN + lax.rem(z, 2) * 64
    tile = jnp.zeros((8, 128), F32)
    for f in range(OWN):
        top = jnp.max(gains[:, f * BINS:(f + 1) * BINS], axis=1, keepdims=True)
        tile = jnp.where((lane == base + f) & (row8 < 2), top, tile)

    pltpu.make_async_copy(yrecv, yrecv, y_recv).wait()
    leaf_sum = ysend[...] + yrecv[0] + yrecv[1] + yrecv[2]
    leaf_sum = jnp.concatenate([jnp.zeros((2, 128), F32), leaf_sum[:6]], axis=0)
    g1[...] = jnp.where(row8 < 2, tile, leaf_sum)

    def g1_copy(r):
        return pltpu.make_async_remote_copy(
            src_ref=g1, dst_ref=g1r.at[NX - r - 1], send_sem=g_send.at[0], recv_sem=g_recv.at[0],
            device_id=xpeer(r), device_id_type=MESH)

    for r in range(1, NX):
        g1_copy(r).start()
    pltpu.make_async_copy(g1r, g1r, g_recv.at[0]).wait()
    whole = g1[...]
    for r in range(NX - 1):
        whole = whole + g1r[r]
    g2[...] = whole

    def g2_copy(r):
        return pltpu.make_async_remote_copy(
            src_ref=g2, dst_ref=g2r.at[NZ - r - 1], send_sem=g_send.at[1], recv_sem=g_recv.at[1],
            device_id=zpeer(r), device_id_type=MESH)

    for r in range(1, NZ):
        g2_copy(r).start()
    pltpu.make_async_copy(g2r, g2r, g_recv.at[1]).wait()
    tiles = [g2[...]] + [g2r[r] for r in range(NZ - 1)]
    for j in range(WIDTH // 128):
        out = jnp.zeros((8, 128), F32)
        for r in range(NZ):
            here = lax.rem(z + r, NZ) // 2 == j
            out = jnp.where(here, out + tiles[r], out)
        best_ref[:, j * 128:(j + 1) * 128] = out[:2]
    summed = tiles[0]
    for r in range(1, NZ):
        summed = summed + tiles[r]
    tot = summed[4:5]
    for n in range(NODES):
        lft = summed[2 + n:3 + n]
        rgt = tot - lft
        for side, part in enumerate((lft, rgt)):
            g = part[:, n * K:(n + 1) * K]
            h = part[:, 32 + n:33 + n]
            leaf_ref[2 * n + side:2 * n + side + 1, :] = -g / (h + LAMBDA_REG)

    for c in first + second:
        c.wait_send()
    for i in range(NZ):
        pltpu.make_async_copy(rx.at[i], rx.at[i], rx_send.at[i]).wait()
    for i in range(NZ - 1):
        pltpu.make_async_copy(rz.at[i], rz.at[i], rz_send.at[i]).wait()
    pltpu.make_async_copy(yrecv, yrecv, y_send).wait()
    pltpu.make_async_copy(g1r, g1r, g_send.at[0]).wait()
    pltpu.make_async_copy(g2r, g2r, g_send.at[1]).wait()


def shards(table, sample_rows, gradients, hessian, node_ids, split_feature, split_bin):
    vmem = pl.BlockSpec(memory_space=pltpu.VMEM)
    smem = pl.BlockSpec(memory_space=pltpu.SMEM)
    dma = pltpu.SemaphoreType.DMA
    return pl.pallas_call(
        kernel,
        out_shape=(
            jax.ShapeDtypeStruct((NODES, WIDTH), F32),
            jax.ShapeDtypeStruct((2 * NODES, K), F32),
        ),
        in_specs=[smem, smem, pl.BlockSpec(memory_space=pl.ANY), vmem, vmem, vmem, vmem],
        out_specs=(vmem, vmem),
        scratch_shapes=[
            pltpu.VMEM((TAB, WIDTH), jnp.int32),
            pltpu.VMEM((WIDTH, S), F32),
            pltpu.VMEM((NZ, NX - 1, OWN, S), F32),
            pltpu.VMEM((NX, 72, 128), F32),
            pltpu.VMEM((NX, 48, S), BF16),
            pltpu.VMEM((NZ, ROWS, LANES), F32),
            pltpu.VMEM((NZ + 1, ROWS, LANES), F32),
            pltpu.VMEM((8, 128), F32),
            pltpu.VMEM((NY - 1, 8, 128), F32),
            pltpu.VMEM((8, 128), F32),
            pltpu.VMEM((NX - 1, 8, 128), F32),
            pltpu.VMEM((8, 128), F32),
            pltpu.VMEM((NZ - 1, 8, 128), F32),
            dma,
            dma((NZ,)), dma((NZ,)),
            dma((7,)), dma((8,)),
            dma((NZ,)), dma((NZ + 1,)),
            dma, dma,
            dma((2,)), dma((2,)),
        ],
        compiler_params=pltpu.CompilerParams(
            collective_id=0, has_side_effects=True, vmem_limit_bytes=48 * 2**20),
    )(
        split_feature, split_bin, table, sample_rows.reshape(1, S), gradients.T,
        hessian.reshape(1, S), node_ids.reshape(1, S),
    )


def solution(mesh):
    return jax.shard_map(
        shards,
        mesh=mesh,
        in_specs=(P("dp", "feat"), P("dp"), P("dp", None), P("dp"), P("dp"), P(), P()),
        out_specs=(P(None, "feat"), P()),
        check_vma=False,
    )
```

```python
import jax
import jax.numpy as jnp
from jax import lax
from jax.experimental import pallas as pl
from jax.experimental.pallas import tpu as pltpu
from jax.sharding import PartitionSpec as P

BINS = 64
K = 16
NODES = 2
LAMBDA_REG = 1.0
GAIN_WEIGHT = 0.01

NX = 8
NZ = 8
NY = 4
S = 512
TAB = 1024
WIDTH = 512
OWN = 8
COLS = WIDTH // 128
WROWS = 48
HROWS = COLS * 32 + 8
FAR = (4, 3, 5, 2, 6, 1, 7, 0)
MESH = pl.DeviceIdType.MESH
F32 = jnp.float32
BF16 = jnp.bfloat16


def iota(shape, dim):
    return lax.broadcasted_iota(jnp.int32, shape, dim)


def choose(i, values):
    out = values[-1]
    for k in range(len(values) - 2, -1, -1):
        out = jnp.where(i == k, values[k], out)
    return out


def nt(a, b):
    return lax.dot_general(a, b, (((1,), (1,)), ((), ())), preferred_element_type=F32)


def kernel(
    sf_hbm, sb_hbm, table_hbm, rows_hbm, grad_hbm, hess_hbm, node_hbm,
    best_ref, leaf_ref,
    sf, sb, tab, rows_v, grad_v, hess_v, node_v, pk, rx, blob, wt, acc, zs, rz,
    lf, lfy, lfx, lfz, fin, fin_own,
    in_sem, tab_sem, rx_send, rx_recv, sib_send, sib_recv, ch_send, ch_recv, rz_send, rz_recv,
    l_send, l_recv, f_send, f_recv,
):
    d = lax.axis_index("dp")
    y = lax.axis_index("feat")
    z = d // NX
    xd = d % NX
    core = xd % 2
    sib_rel = 1 - 2 * core

    def xpeer(r):
        return (z * NX + lax.rem(xd + r, NX), y)

    def zpeer(q):
        return (lax.rem(z + q, NZ) * NX + xd, y)

    def ypeer(r):
        return (d, lax.rem(y + r, NY))

    sibling = (d + sib_rel, y)

    ins = [
        pltpu.make_async_copy(src, dst, in_sem.at[k])
        for k, (src, dst) in enumerate((
            (rows_hbm, rows_v), (grad_hbm, grad_v), (hess_hbm, hess_v), (node_hbm, node_v),
            (sf_hbm, sf), (sb_hbm, sb)))
    ]
    ins[0].start()
    first_col = lax.rem(z // 2 + 2, COLS)

    def col(j):
        return pl.multiple_of(lax.rem(first_col + j, COLS) * 128, 128)

    loads = [
        pltpu.make_async_copy(
            table_hbm.at[:, pl.ds(col(j), 128)], tab.at[j], tab_sem.at[j])
        for j in range(COLS)
    ]
    for c in loads:
        c.start()
    for c in ins[1:]:
        c.start()

    barrier = pltpu.get_barrier_semaphore()
    for r in FAR[:-1]:
        pl.semaphore_signal(barrier, inc=1, device_id=zpeer(r), device_id_type=MESH)
    for r in range(1, NX):
        pl.semaphore_signal(barrier, inc=1, device_id=xpeer(r), device_id_type=MESH)
    for r in range(1, NY):
        pl.semaphore_signal(barrier, inc=1, device_id=ypeer(r), device_id_type=MESH)

    for c in ins[1:]:
        c.wait()
    for j in range(COLS):
        lanes = slice(j * 128, (j + 1) * 128)
        blob[0, j * K:(j + 1) * K, :] = grad_v[:, lanes].astype(F32)
        blob[0, 64 + 2 * j:65 + 2 * j, :] = hess_v[j:j + 1, :].astype(F32)
        blob[0, 65 + 2 * j:66 + 2 * j, :] = node_v[:, lanes].astype(F32)

    ins[0].wait()
    hot = jnp.where(iota((TAB, S), 0) == rows_v[...], 1.0, 0.0).astype(BF16)

    for j in range(COLS):
        loads[j].wait()
        part = tab[j].astype(F32).astype(BF16)
        pk[pl.ds(col(j), 128), :] = lax.dot_general(
            part, hot, (((0,), (0,)), ((), ())), preferred_element_type=F32)

    pl.semaphore_wait(barrier, NX + NZ + NY - 3)

    def ch_copy(src_slot, dst_slot, where, k):
        return pltpu.make_async_remote_copy(
            src_ref=blob.at[src_slot], dst_ref=blob.at[dst_slot],
            send_sem=ch_send.at[k], recv_sem=ch_recv.at[dst_slot],
            device_id=where, device_id_type=MESH,
        )

    first = [ch_copy(0, 4 - m, xpeer(2 * m), m) for m in range(1, 4)] + [ch_copy(0, 4, sibling, 0)]
    for c in first:
        c.start()

    def chunk_z(i):
        return lax.rem(z + choose(i, (3, 5, 4, 2, 6, 1, 7, 0)), NZ)

    def x_copy(i, m, other):
        peer_x = lax.rem(xd + 2 * m + NX, NX)
        peer_x = jnp.where(other, peer_x + sib_rel, peer_x) if other else peer_x
        row = pl.multiple_of(chunk_z(i) * (NX * OWN) + peer_x * OWN, OWN)
        if m == 0:
            send, recv, slot = sib_send, sib_recv, 0
        else:
            send, recv, slot = rx_send.at[i], rx_recv.at[i], (3 if other else 0) + 4 - m
        return pltpu.make_async_remote_copy(
            src_ref=pk.at[pl.ds(row, OWN), :],
            dst_ref=rx.at[slot, i],
            send_sem=send, recv_sem=recv,
            device_id=(z * NX + peer_x, y), device_id_type=MESH,
        )

    def weights(slot, place):
        for j in range(COLS):
            g = blob[slot, j * K:(j + 1) * K, :]
            h = blob[slot, 64 + 2 * j:65 + 2 * j, :]
            n = blob[slot, 65 + 2 * j:66 + 2 * j, :]
            at0 = n == 0.0
            at1 = n == 1.0
            rest = jnp.where(iota((16, 128), 0) == 0, jnp.where(at0, h, 0.0),
                             jnp.where(iota((16, 128), 0) == 1, jnp.where(at1, h, 0.0), 0.0))
            full = jnp.concatenate(
                [jnp.where(at0, g, 0.0), jnp.where(at1, g, 0.0), rest], axis=0)
            wt[place, :, j * 128:(j + 1) * 128] = full.astype(BF16)

    level = iota((BINS, S), 0).astype(F32).astype(BF16)
    one = jnp.ones((), BF16)
    zero = jnp.zeros((), BF16)

    def below(value):
        return jnp.where(jnp.broadcast_to(value.astype(BF16), (BINS, S)) <= level, one, zero)

    def product(place, values):
        return nt(wt[place], jnp.concatenate([below(v) for v in values], axis=0))

    weights(0, 0)

    def own_chunk(i, carry):
        for m in (2, 1, 3):
            x_copy(i, m, False).start()
            x_copy(i, m, True).start()
        x_copy(i, 0, True).start()
        mine = chunk_z(i) * (NX * OWN) + xd * OWN
        acc[i] = product(0, [pk[pl.ds(mine + f, 1), :] for f in range(OWN)])
        return carry

    lax.fori_loop(0, NZ, own_chunk, 0)

    sides = []
    for n in range(NODES):
        at = sf[n] - y * WIDTH
        inside = jnp.where((at >= 0) & (at < WIDTH), 1.0, 0.0).astype(F32)
        row = pk[pl.ds(jnp.clip(at, 0, WIDTH - 1), 1), :]
        sides.append(jnp.where(row <= sb[n].astype(F32), inside, 0.0))
    ind = jnp.concatenate([
        jnp.where(node_v[...] == 0, sides[0], sides[1]),
        jnp.full((1, S), jnp.where(y == 0, 1.0, 0.0).astype(F32)),
        jnp.zeros((14, S), F32)], axis=0).astype(BF16)
    part = nt(ind, wt[0])
    gap = jnp.zeros((1, 64 - WROWS), F32)
    lf[0] = jnp.concatenate([part[:1], gap, part[1:2], gap], axis=1)

    def l_copy(stage, dst, where):
        return pltpu.make_async_remote_copy(
            src_ref=lf.at[stage], dst_ref=dst, send_sem=l_send.at[stage], recv_sem=l_recv.at[stage],
            device_id=where, device_id_type=MESH)

    for r in range(1, NY):
        l_copy(0, lfy.at[NY - r - 1], ypeer(r)).start()

    for c in first[:3]:
        c.wait_recv()
    second = [ch_copy(m, 4 + m, sibling, 3 + m) for m in range(1, 4)]
    for c in second:
        c.start()

    first[3].wait_recv()
    weights(4, 4)
    pltpu.make_async_copy(rx.at[0], rx.at[0], sib_recv).wait()

    def sib_chunk(i, carry):
        acc[i] += product(4, [rx[0, i, f:f + 1, :] for f in range(OWN)])
        return carry

    lax.fori_loop(0, NZ, sib_chunk, 0)

    for m in range(1, 4):
        weights(m, m)
    for c in second:
        c.wait_recv()
    for m in range(5, 8):
        weights(m, m)

    def z_copy(i):
        dz = choose(i, (1, 7, 4, 2, 6, 1, 7))
        return pltpu.make_async_remote_copy(
            src_ref=zs.at[i], dst_ref=rz.at[i],
            send_sem=rz_send.at[i], recv_sem=rz_recv.at[i],
            device_id=(lax.rem(z + dz, NZ) * NX + xd, y), device_id_type=MESH,
        )

    def chunk(i, carry):
        six = rx.at[pl.ds(1, 6), 0]
        pltpu.make_async_copy(six, six, rx_recv.at[i]).wait()
        total = acc[i]
        for slot in range(1, 7):
            place = slot if slot < 4 else slot + 1
            total = total + product(place, [rx[slot, i, f:f + 1, :] for f in range(OWN)])
        for j in range(COLS):
            lanes = slice(j * 128, (j + 1) * 128)
            zs[i, j * 32:(j + 1) * 32, :] = total[:32, lanes]
            zs[i, 128 + 2 * j:130 + 2 * j, :] = total[32:34, lanes]

        @pl.when((i == 3) | (i == 4))
        def _():
            pltpu.make_async_copy(rz.at[i - 3], rz.at[i - 3], rz_recv.at[i - 3]).wait()
            zs[i] = zs[i] + rz[i - 3]

        @pl.when(i < NZ - 1)
        def _():
            z_copy(i).start()

        @pl.when(i == 1)
        def _():
            pltpu.make_async_copy(lfy, lfy, l_recv.at[0]).wait()
            lf[1] = lf[0] + lfy[0] + lfy[1] + lfy[2]
            for r in range(1, NX):
                l_copy(1, lfx.at[NX - r - 1], xpeer(r)).start()

        @pl.when(i == 4)
        def _():
            pltpu.make_async_copy(lfx, lfx, l_recv.at[1]).wait()
            s = lf[1]
            for r in range(NX - 1):
                s = s + lfx[r]
            lf[2] = s
            for r in range(1, NZ):
                l_copy(2, lfz.at[NZ - r - 1], zpeer(r)).start()

        return carry

    lax.fori_loop(0, NZ, chunk, 0)
    pltpu.make_async_copy(lfz, lfz, l_recv.at[2]).wait()
    for i in range(2, 7):
        pltpu.make_async_copy(rz.at[i], rz.at[i], rz_recv.at[i]).wait()
    left = zs[7] + rz[2] + rz[3] + rz[4] + rz[5] + rz[6]

    tot_g = jnp.broadcast_to(left[:32, BINS - 1:BINS], (32, 128))
    tot_h = jnp.broadcast_to(left[128:130, BINS - 1:BINS], (2, 128))

    def score(g, h):
        return jnp.sum(g * g, axis=0, keepdims=True) / (h + LAMBDA_REG)

    gains = []
    for j in range(COLS):
        for n in range(NODES):
            gl = left[j * 32 + n * K:j * 32 + (n + 1) * K]
            hl = left[128 + 2 * j + n:129 + 2 * j + n]
            gt = tot_g[n * K:(n + 1) * K]
            ht = tot_h[n:n + 1]
            gains.append(score(gl, hl) + score(gt - gl, ht - hl) - score(gt, ht))
    gains = jnp.concatenate(gains, axis=0) * (GAIN_WEIGHT / K)
    lane = iota((8, 128), 1)
    row8 = iota((8, 128), 0)
    low = jnp.max(jnp.where(lane < BINS, gains, -jnp.inf), axis=1, keepdims=True)
    high = jnp.max(jnp.where(lane >= BINS, gains, -jnp.inf), axis=1, keepdims=True)
    home = lax.rem(row8 + z, 2) * 64 + xd * OWN + (row8 // 2) * 2
    mine = jnp.where(lane == home, low, jnp.where(lane == home + 1, high, 0.0))
    mine = jnp.sum(mine, axis=0, keepdims=True)
    fin_own[...] = mine
    fin[d] = mine

    def f_copy(q, r):
        return pltpu.make_async_remote_copy(
            src_ref=fin_own, dst_ref=fin.at[d], send_sem=f_send, recv_sem=f_recv,
            device_id=(lax.rem(z + q, NZ) * NX + lax.rem(xd + r, NX), y), device_id_type=MESH)

    pairs = [(q, r) for q in FAR for r in FAR if q or r]
    for q, r in pairs:
        f_copy(q, r).start()

    s = lf[2]
    for r in range(NZ - 1):
        s = s + lfz[r]
    for n in range(NODES):
        tot = s[:, 64:128]
        lft = s[:, 0:64]
        for side, part in enumerate((lft, tot - lft)):
            g = part[:, n * K:(n + 1) * K]
            h = part[:, 32 + n:33 + n]
            leaf_ref[2 * n + side:2 * n + side + 1, :] = -g / (h + LAMBDA_REG)

    for c in first + second:
        c.wait_send()
    six = rx.at[pl.ds(1, 6), 0]
    for i in range(NZ):
        pltpu.make_async_copy(six, six, rx_send.at[i]).wait()
    pltpu.make_async_copy(rx.at[0], rx.at[0], sib_send).wait()
    for i in range(NZ - 1):
        pltpu.make_async_copy(rz.at[i], rz.at[i], rz_send.at[i]).wait()
    pltpu.make_async_copy(lfy, lfy, l_send.at[0]).wait()
    pltpu.make_async_copy(lfx, lfx, l_send.at[1]).wait()
    pltpu.make_async_copy(lfz, lfz, l_send.at[2]).wait()

    others = fin.at[pl.ds(0, NX * NZ - 1)]
    pltpu.make_async_copy(others, others, f_recv).wait()
    lane1 = iota((1, 128), 1)
    for j in range(COLS):
        pair = []
        for q in (2 * j, 2 * j + 1):
            v = fin[q * NX]
            for r in range(1, NX):
                v = v + fin[q * NX + r]
            pair.append(v)
        best_ref[0:1, j * 128:(j + 1) * 128] = jnp.where(lane1 < 64, pair[0], pair[1])
        best_ref[1:2, j * 128:(j + 1) * 128] = pltpu.roll(
            jnp.where(lane1 < 64, pair[1], pair[0]), 64, axis=1)
    pltpu.make_async_copy(others, others, f_send).wait()


def shards(table, sample_rows, gradients, hessian, node_ids, split_feature, split_bin):
    vmem = pl.BlockSpec(memory_space=pltpu.VMEM)
    hbm = pl.BlockSpec(memory_space=pltpu.HBM)
    dma = pltpu.SemaphoreType.DMA
    row = pltpu.VMEM((1, 128), F32)
    return pl.pallas_call(
        kernel,
        out_shape=(
            jax.ShapeDtypeStruct((NODES, WIDTH), F32),
            jax.ShapeDtypeStruct((2 * NODES, K), F32),
        ),
        in_specs=[hbm] * 7,
        out_specs=(vmem, vmem),
        scratch_shapes=[
            pltpu.SMEM((NODES,), jnp.int32),
            pltpu.SMEM((NODES,), jnp.int32),
            pltpu.VMEM((COLS, TAB, 128), jnp.int32),
            pltpu.VMEM((1, S), jnp.int32),
            pltpu.VMEM((K, S), BF16),
            pltpu.VMEM((COLS, 128), BF16),
            pltpu.VMEM((1, S), jnp.int32),
            pltpu.VMEM((WIDTH, S), F32),
            pltpu.VMEM((NX - 1, NZ, OWN, S), F32),
            pltpu.VMEM((NX, 72, 128), F32),
            pltpu.VMEM((NX, WROWS, S), BF16),
            pltpu.VMEM((NZ, WROWS, OWN * BINS), F32),
            pltpu.VMEM((NZ, HROWS, 128), F32),
            pltpu.VMEM((NZ - 1, HROWS, 128), F32),
            pltpu.VMEM((3, 1, 128), F32),
            pltpu.VMEM((NY - 1, 1, 128), F32),
            pltpu.VMEM((NX - 1, 1, 128), F32),
            pltpu.VMEM((NZ - 1, 1, 128), F32),
            pltpu.VMEM((NX * NZ, 1, 128), F32),
            row,
            dma((6,)), dma((COLS,)),
            dma((NZ,)), dma((NZ,)),
            dma, dma,
            dma((7,)), dma((8,)),
            dma((NZ - 1,)), dma((NZ - 1,)),
            dma((3,)), dma((3,)),
            dma, dma,
        ],
        compiler_params=pltpu.CompilerParams(
            collective_id=0, has_side_effects=True, vmem_limit_bytes=60 * 2**20),
    )(
        split_feature, split_bin, table, sample_rows.reshape(1, S), gradients.T,
        hessian.reshape(COLS, 128), node_ids.reshape(1, S),
    )


def solution(mesh):
    return jax.shard_map(
        shards,
        mesh=mesh,
        in_specs=(P("dp", "feat"), P("dp"), P("dp", None), P("dp"), P("dp"), P(), P()),
        out_specs=(P(None, "feat"), P()),
        check_vma=False,
    )
```

```python
import jax
import jax.numpy as jnp
from jax import lax
from jax.experimental import pallas as pl
from jax.experimental.pallas import tpu as pltpu
from jax.sharding import PartitionSpec as P

BINS = 64
K = 16
NODES = 2
LAMBDA_REG = 1.0
GAIN_WEIGHT = 0.01

NX = 8
NZ = 8
NY = 4
S = 512
TAB = 1024
WIDTH = 512
OWN = 8
COLS = WIDTH // 128
WROWS = 48
HROWS = COLS * 32 + 8
AHEAD = 3
FAR = (4, 3, 5, 2, 6, 1, 7, 0)
MESH = pl.DeviceIdType.MESH
F32 = jnp.float32
BF16 = jnp.bfloat16


def iota(shape, dim):
    return lax.broadcasted_iota(jnp.int32, shape, dim)


def choose(i, values):
    out = values[-1]
    for k in range(len(values) - 2, -1, -1):
        out = jnp.where(i == k, values[k], out)
    return out


def nt(a, b):
    return lax.dot_general(a, b, (((1,), (1,)), ((), ())), preferred_element_type=F32)


def kernel(
    sf_hbm, sb_hbm, table_hbm, rows_hbm, grad_hbm, hess_hbm, node_hbm,
    fin, leaf_sum,
    sf, sb, tab, rows_v, grad_v, hess_v, node_v, pk, rx, blob, wt, acc, zs, rz,
    lf, lfy, lfx, lfz, fin_own, leaf_v,
    in_sem, tab_sem, rx_send, rx_recv, sib_send, sib_recv, ch_send, ch_recv, rz_send, rz_recv,
    l_send, l_recv, f_send, f_recv, out_sem, hello,
):
    d = lax.axis_index("dp")
    y = lax.axis_index("feat")
    z = d // NX
    xd = d % NX
    core = xd % 2
    sib_rel = 1 - 2 * core
    turn = 1 - 2 * lax.rem(z, 2)

    def xpeer(r):
        return (z * NX + lax.rem(xd + r, NX), y)

    def zpeer(q):
        return (lax.rem(z + q, NZ) * NX + xd, y)

    def ypeer(r):
        return (d, lax.rem(y + r, NY))

    sibling = (d + sib_rel, y)

    ins = [
        pltpu.make_async_copy(src, dst, in_sem.at[k])
        for k, (src, dst) in enumerate((
            (rows_hbm, rows_v), (grad_hbm, grad_v), (hess_hbm, hess_v), (node_hbm, node_v),
            (sf_hbm, sf), (sb_hbm, sb)))
    ]
    ins[0].start()

    def col(j):
        ahead = (2, 2 - turn, 2 + turn, 0)[j]
        return pl.multiple_of(lax.rem(z // 2 + ahead, COLS) * 128, 128)

    loads = [
        pltpu.make_async_copy(
            table_hbm.at[:, pl.ds(col(j), 128)], tab.at[j], tab_sem.at[j])
        for j in range(COLS)
    ]
    for c in loads:
        c.start()
    for c in ins[1:]:
        c.start()

    barrier = pltpu.get_barrier_semaphore()
    for r in (1, NZ - 1):
        pl.semaphore_signal(barrier, inc=1, device_id=zpeer(r), device_id_type=MESH)
    for r in range(1, NX):
        pl.semaphore_signal(barrier, inc=1, device_id=xpeer(r), device_id_type=MESH)
    for r in range(1, NY):
        pl.semaphore_signal(barrier, inc=1, device_id=ypeer(r), device_id_type=MESH)

    def greet(k):
        for r in (1, NZ - 1):
            pl.semaphore_signal(hello.at[k], inc=1, device_id=zpeer(r), device_id_type=MESH)

    def greeted(k):
        pl.semaphore_wait(hello.at[k], 2)

    for c in ins[1:]:
        c.wait()
    for j in range(COLS):
        lanes = slice(j * 128, (j + 1) * 128)
        blob[0, j * K:(j + 1) * K, :] = grad_v[:, lanes].astype(F32)
        blob[0, 64 + 2 * j:65 + 2 * j, :] = hess_v[j:j + 1, :].astype(F32)
        blob[0, 65 + 2 * j:66 + 2 * j, :] = node_v[:, lanes].astype(F32)

    ins[0].wait()
    hot = jnp.where(iota((TAB, S), 0) == rows_v[...], 1.0, 0.0).astype(BF16)

    def ch_copy(src_slot, dst_slot, where, k):
        return pltpu.make_async_remote_copy(
            src_ref=blob.at[src_slot], dst_ref=blob.at[dst_slot],
            send_sem=ch_send.at[k], recv_sem=ch_recv.at[dst_slot],
            device_id=where, device_id_type=MESH,
        )

    first = [ch_copy(0, 4 - m, xpeer(2 * m), m) for m in range(1, 4)] + [ch_copy(0, 4, sibling, 0)]

    def chunk_z(i):
        return lax.rem(z + NZ + choose(i, (4, -3 * turn, 3 * turn, 2 * turn, -2 * turn, -turn, turn, 0)), NZ)

    def x_copy(i, m, other):
        peer_x = lax.rem(xd + 2 * m + NX, NX)
        peer_x = jnp.where(other, peer_x + sib_rel, peer_x) if other else peer_x
        row = pl.multiple_of(chunk_z(i) * (NX * OWN) + peer_x * OWN, OWN)
        if m == 0:
            send, recv, slot = sib_send, sib_recv, 0
        else:
            send, recv, slot = rx_send.at[i], rx_recv.at[i], (3 if other else 0) + 4 - m
        return pltpu.make_async_remote_copy(
            src_ref=pk.at[pl.ds(row, OWN), :],
            dst_ref=rx.at[slot, i],
            send_sem=send, recv_sem=recv,
            device_id=(z * NX + peer_x, y), device_id_type=MESH,
        )

    def start_chunk(i):
        for m in (2, 1, 3):
            x_copy(i, m, False).start()
            x_copy(i, m, True).start()

    for j in range(COLS):
        loads[j].wait()
        part = tab[j].astype(F32).astype(BF16)
        pk[pl.ds(col(j), 128), :] = lax.dot_general(
            part, hot, (((0,), (0,)), ((), ())), preferred_element_type=F32)
        if j == 0:
            pl.semaphore_wait(barrier, NX + NY)
            for c in first:
                c.start()
        for i in (2 * j, 2 * j + 1):
            if i < AHEAD:
                start_chunk(i)
            x_copy(i, 0, True).start()
        if j == 0:
            greet(0)
        if j == 2:
            greeted(0)
            greet(1)

    def weights(slot, place):
        for j in range(COLS):
            g = blob[slot, j * K:(j + 1) * K, :]
            h = blob[slot, 64 + 2 * j:65 + 2 * j, :]
            n = blob[slot, 65 + 2 * j:66 + 2 * j, :]
            at0 = n == 0.0
            at1 = n == 1.0
            rest = jnp.where(iota((16, 128), 0) == 0, jnp.where(at0, h, 0.0),
                             jnp.where(iota((16, 128), 0) == 1, jnp.where(at1, h, 0.0), 0.0))
            full = jnp.concatenate(
                [jnp.where(at0, g, 0.0), jnp.where(at1, g, 0.0), rest], axis=0)
            wt[place, :, j * 128:(j + 1) * 128] = full.astype(BF16)

    level = iota((BINS, S), 0).astype(F32).astype(BF16)
    one = jnp.ones((), BF16)
    zero = jnp.zeros((), BF16)

    def below(value):
        return jnp.where(jnp.broadcast_to(value.astype(BF16), (BINS, S)) <= level, one, zero)

    def product(place, values):
        return nt(wt[place], jnp.concatenate([below(v) for v in values], axis=0))

    weights(0, 0)

    def own_chunk(i, carry):
        mine = chunk_z(i) * (NX * OWN) + xd * OWN
        acc[i] = product(0, [pk[pl.ds(mine + f, 1), :] for f in range(OWN)])
        return carry

    lax.fori_loop(0, NZ, own_chunk, 0)

    greeted(1)
    greet(2)

    sides = []
    for n in range(NODES):
        at = sf[n] - y * WIDTH
        inside = jnp.where((at >= 0) & (at < WIDTH), 1.0, 0.0).astype(F32)
        row = pk[pl.ds(jnp.clip(at, 0, WIDTH - 1), 1), :]
        sides.append(jnp.where(row <= sb[n].astype(F32), inside, 0.0))
    ind = jnp.concatenate([
        jnp.where(node_v[...] == 0, sides[0], sides[1]),
        jnp.full((1, S), jnp.where(y == 0, 1.0, 0.0).astype(F32)),
        jnp.zeros((14, S), F32)], axis=0).astype(BF16)
    part = nt(ind, wt[0])
    gap = jnp.zeros((1, 64 - WROWS), F32)
    lf[0] = jnp.concatenate([part[:1], gap, part[1:2], gap], axis=1)

    def l_copy(stage, dst, where):
        return pltpu.make_async_remote_copy(
            src_ref=lf.at[stage], dst_ref=dst, send_sem=l_send.at[stage], recv_sem=l_recv.at[stage],
            device_id=where, device_id_type=MESH)

    for r in range(1, NY):
        l_copy(0, lfy.at[NY - r - 1], ypeer(r)).start()

    for c in first[:3]:
        c.wait_recv()
    second = [ch_copy(m, 4 + m, sibling, 3 + m) for m in range(1, 4)]
    for c in second:
        c.start()

    first[3].wait_recv()
    weights(4, 4)
    pltpu.make_async_copy(rx.at[0], rx.at[0], sib_recv).wait()

    def sib_chunk(i, carry):
        acc[i] += product(4, [rx[0, i, f:f + 1, :] for f in range(OWN)])
        return carry

    lax.fori_loop(0, NZ, sib_chunk, 0)

    for m in range(1, 4):
        weights(m, m)
    for c in second:
        c.wait_recv()
    for m in range(5, 8):
        weights(m, m)
    greeted(2)

    def z_copy(i):
        dz = choose(i, (-turn, -turn, turn, 2 * turn, -2 * turn, -turn, turn))
        return pltpu.make_async_remote_copy(
            src_ref=zs.at[i], dst_ref=rz.at[i],
            send_sem=rz_send.at[i], recv_sem=rz_recv.at[i],
            device_id=(lax.rem(z + NZ + dz, NZ) * NX + xd, y), device_id_type=MESH,
        )

    def chunk(i, carry):
        @pl.when(i + AHEAD < NZ)
        def _():
            start_chunk(i + AHEAD)

        six = rx.at[pl.ds(1, 6), 0]
        pltpu.make_async_copy(six, six, rx_recv.at[i]).wait()
        total = acc[i]
        for slot in range(1, 7):
            place = slot if slot < 4 else slot + 1
            total = total + product(place, [rx[slot, i, f:f + 1, :] for f in range(OWN)])
        for j in range(COLS):
            lanes = slice(j * 128, (j + 1) * 128)
            zs[i, j * 32:(j + 1) * 32, :] = total[:32, lanes]
            zs[i, 128 + 2 * j:130 + 2 * j, :] = total[32:34, lanes]

        @pl.when((i < 2) | (i == 5) | (i == 6))
        def _():
            z_copy(i).start()

        @pl.when((i == 3) | (i == 4) | (i == 6))
        def _():
            c = jnp.where(i == 6, 4, i - 1)
            pltpu.make_async_copy(rz.at[c - 2], rz.at[c - 2], rz_recv.at[c - 2]).wait()
            zs[c] = zs[c] + rz[c - 2]
            z_copy(c).start()

        @pl.when(i == 1)
        def _():
            pltpu.make_async_copy(lfy, lfy, l_recv.at[0]).wait()
            lf[1] = lf[0] + lfy[0] + lfy[1] + lfy[2]
            for r in range(1, NX):
                l_copy(1, lfx.at[NX - r - 1], xpeer(r)).start()

        @pl.when(i == 4)
        def _():
            pltpu.make_async_copy(lfx, lfx, l_recv.at[1]).wait()
            s = lf[1]
            for r in range(NX - 1):
                s = s + lfx[r]
            lf[2] = s
            for r in range(1, NZ):
                l_copy(2, lfz.at[NZ - r - 1], zpeer(r)).start()

        return carry

    lax.fori_loop(0, NZ, chunk, 0)
    pltpu.make_async_copy(lfz, lfz, l_recv.at[2]).wait()
    for i in (3, 4, 5, 6):
        pltpu.make_async_copy(rz.at[i], rz.at[i], rz_recv.at[i]).wait()
    left = zs[7] + rz[3] + rz[4] + rz[5] + rz[6]

    tot_g = jnp.broadcast_to(left[:32, BINS - 1:BINS], (32, 128))
    tot_h = jnp.broadcast_to(left[128:130, BINS - 1:BINS], (2, 128))

    def score(g, h):
        return jnp.sum(g * g, axis=0, keepdims=True) / (h + LAMBDA_REG)

    gains = []
    for j in range(COLS):
        for n in range(NODES):
            gl = left[j * 32 + n * K:j * 32 + (n + 1) * K]
            hl = left[128 + 2 * j + n:129 + 2 * j + n]
            gt = tot_g[n * K:(n + 1) * K]
            ht = tot_h[n:n + 1]
            gains.append(score(gl, hl) + score(gt - gl, ht - hl) - score(gt, ht))
    gains = jnp.concatenate(gains, axis=0) * (GAIN_WEIGHT / K)
    lane = iota((8, 128), 1)
    row8 = iota((8, 128), 0)
    low = jnp.max(jnp.where(lane < BINS, gains, -jnp.inf), axis=1, keepdims=True)
    high = jnp.max(jnp.where(lane >= BINS, gains, -jnp.inf), axis=1, keepdims=True)
    home = lax.rem(row8 + z, 2) * 64 + xd * OWN + (row8 // 2) * 2
    mine = jnp.where(lane == home, low, jnp.where(lane == home + 1, high, 0.0))
    mine = jnp.sum(mine, axis=0, keepdims=True)
    fin_own[...] = mine
    keep = pltpu.make_async_copy(fin_own, fin.at[d], out_sem.at[0])
    keep.start()

    def f_copy(to_z, r):
        return pltpu.make_async_remote_copy(
            src_ref=fin_own, dst_ref=fin.at[d], send_sem=f_send, recv_sem=f_recv,
            device_id=(to_z * NX + lax.rem(xd + r, NX), y), device_id_type=MESH)

    for to_z in range(NZ):
        for r in FAR[:-1]:
            f_copy(to_z, r).start()

        @pl.when(z != to_z)
        def _():
            f_copy(to_z, 0).start()

    s = lf[2]
    for r in range(NZ - 1):
        s = s + lfz[r]
    leaf_v[...] = s
    keep_leaf = pltpu.make_async_copy(leaf_v, leaf_sum, out_sem.at[1])
    keep_leaf.start()

    for c in first + second:
        c.wait_send()
    six = rx.at[pl.ds(1, 6), 0]
    for i in range(NZ):
        pltpu.make_async_copy(six, six, rx_send.at[i]).wait()
    pltpu.make_async_copy(rx.at[0], rx.at[0], sib_send).wait()
    for i in range(NZ - 1):
        pltpu.make_async_copy(rz.at[i], rz.at[i], rz_send.at[i]).wait()
    pltpu.make_async_copy(lfy, lfy, l_send.at[0]).wait()
    pltpu.make_async_copy(lfx, lfx, l_send.at[1]).wait()
    pltpu.make_async_copy(lfz, lfz, l_send.at[2]).wait()

    others = fin.at[pl.ds(0, NX * NZ - 1)]
    pltpu.make_async_copy(others, others, f_recv).wait()
    pltpu.make_async_copy(others, others, f_send).wait()
    keep.wait()
    keep_leaf.wait()


def assemble(fin, leaf_sum, best_ref, leaf_ref):
    lane = iota((1, 128), 1)
    for j in range(COLS):
        pair = []
        for q in (2 * j, 2 * j + 1):
            v = fin[q * NX]
            for r in range(1, NX):
                v = v + fin[q * NX + r]
            pair.append(v)
        best_ref[0:1, j * 128:(j + 1) * 128] = jnp.where(lane < 64, pair[0], pair[1])
        best_ref[1:2, j * 128:(j + 1) * 128] = pltpu.roll(
            jnp.where(lane < 64, pair[1], pair[0]), 64, axis=1)
    s = leaf_sum[...]
    tot = s[:, 64:128]
    lft = s[:, 0:64]
    for n in range(NODES):
        for side, part in enumerate((lft, tot - lft)):
            g = part[:, n * K:(n + 1) * K]
            h = part[:, 32 + n:33 + n]
            leaf_ref[2 * n + side:2 * n + side + 1, :] = -g / (h + LAMBDA_REG)


def shards(table, sample_rows, gradients, hessian, node_ids, split_feature, split_bin):
    vmem = pl.BlockSpec(memory_space=pltpu.VMEM)
    hbm = pl.BlockSpec(memory_space=pltpu.HBM)
    dma = pltpu.SemaphoreType.DMA
    row = pltpu.VMEM((1, 128), F32)
    fin, leaf_sum = pl.pallas_call(
        kernel,
        out_shape=(
            jax.ShapeDtypeStruct((NX * NZ, 1, 128), F32),
            jax.ShapeDtypeStruct((1, 128), F32),
        ),
        in_specs=[hbm] * 7,
        out_specs=(hbm, hbm),
        scratch_shapes=[
            pltpu.SMEM((NODES,), jnp.int32),
            pltpu.SMEM((NODES,), jnp.int32),
            pltpu.VMEM((COLS, TAB, 128), jnp.int32),
            pltpu.VMEM((1, S), jnp.int32),
            pltpu.VMEM((K, S), BF16),
            pltpu.VMEM((COLS, 128), BF16),
            pltpu.VMEM((1, S), jnp.int32),
            pltpu.VMEM((WIDTH, S), F32),
            pltpu.VMEM((NX - 1, NZ, OWN, S), F32),
            pltpu.VMEM((NX, 72, 128), F32),
            pltpu.VMEM((NX, WROWS, S), BF16),
            pltpu.VMEM((NZ, WROWS, OWN * BINS), F32),
            pltpu.VMEM((NZ, HROWS, 128), F32),
            pltpu.VMEM((NZ - 1, HROWS, 128), F32),
            pltpu.VMEM((3, 1, 128), F32),
            pltpu.VMEM((NY - 1, 1, 128), F32),
            pltpu.VMEM((NX - 1, 1, 128), F32),
            pltpu.VMEM((NZ - 1, 1, 128), F32),
            row,
            row,
            dma((6,)), dma((COLS,)),
            dma((NZ,)), dma((NZ,)),
            dma, dma,
            dma((7,)), dma((8,)),
            dma((NZ - 1,)), dma((NZ - 1,)),
            dma((3,)), dma((3,)),
            dma, dma,
            dma((2,)),
            pltpu.SemaphoreType.REGULAR((3,)),
        ],
        compiler_params=pltpu.CompilerParams(
            collective_id=0, has_side_effects=True, vmem_limit_bytes=60 * 2**20),
    )(
        split_feature, split_bin, table, sample_rows.reshape(1, S), gradients.T,
        hessian.reshape(COLS, 128), node_ids.reshape(1, S),
    )
    return pl.pallas_call(
        assemble,
        out_shape=(
            jax.ShapeDtypeStruct((NODES, WIDTH), F32),
            jax.ShapeDtypeStruct((2 * NODES, K), F32),
        ),
        in_specs=[vmem, vmem],
        out_specs=(vmem, vmem),
        compiler_params=pltpu.CompilerParams(vmem_limit_bytes=60 * 2**20),
    )(fin, leaf_sum)


def solution(mesh):
    return jax.shard_map(
        shards,
        mesh=mesh,
        in_specs=(P("dp", "feat"), P("dp"), P("dp", None), P("dp"), P("dp"), P(), P()),
        out_specs=(P(None, "feat"), P()),
        check_vma=False,
    )
```

```python
import jax
import jax.numpy as jnp
from jax import lax
from jax.experimental import pallas as pl
from jax.experimental.pallas import tpu as pltpu
from jax.sharding import PartitionSpec as P

BINS = 64
K = 16
NODES = 2
LAMBDA_REG = 1.0
GAIN_WEIGHT = 0.01

NX = 8
NZ = 8
NY = 4
S = 512
TAB = 1024
WIDTH = 512
OWN = 8
COLS = WIDTH // 128
WROWS = 48
HROWS = COLS * 32 + 8
AHEAD = 4
FAR = (4, 3, 5, 2, 6, 1, 7, 0)
MESH = pl.DeviceIdType.MESH
F32 = jnp.float32
BF16 = jnp.bfloat16


def iota(shape, dim):
    return lax.broadcasted_iota(jnp.int32, shape, dim)


def choose(i, values):
    out = values[-1]
    for k in range(len(values) - 2, -1, -1):
        out = jnp.where(i == k, values[k], out)
    return out


def nt(a, b):
    return lax.dot_general(a, b, (((1,), (1,)), ((), ())), preferred_element_type=F32)


def kernel(
    sf_hbm, sb_hbm, table_hbm, rows_hbm, grad_hbm, hess_hbm, node_hbm,
    fin, leaf_sum,
    sf, sb, tab, rows_v, grad_v, hess_v, node_v, pk, rx, blob, wt, acc, zs, rz,
    lf, lfy, lfx, lfz, fin_own, leaf_v,
    in_sem, tab_sem, rx_send, rx_recv, sib_send, sib_recv, ch_send, ch_recv, rz_send, rz_recv,
    l_send, l_recv, f_send, f_recv, out_sem, hello,
):
    d = lax.axis_index("dp")
    y = lax.axis_index("feat")
    z = d // NX
    xd = d % NX
    core = xd % 2
    sib_rel = 1 - 2 * core
    turn = 1 - 2 * lax.rem(z, 2)

    def xpeer(r):
        return (z * NX + lax.rem(xd + r, NX), y)

    def zpeer(q):
        return (lax.rem(z + q, NZ) * NX + xd, y)

    def ypeer(r):
        return (d, lax.rem(y + r, NY))

    sibling = (d + sib_rel, y)

    ins = [
        pltpu.make_async_copy(src, dst, in_sem.at[k])
        for k, (src, dst) in enumerate((
            (rows_hbm, rows_v), (grad_hbm, grad_v), (hess_hbm, hess_v), (node_hbm, node_v),
            (sf_hbm, sf), (sb_hbm, sb)))
    ]
    ins[0].start()

    def col(j):
        ahead = (2, 2 - turn, 2 + turn, 0)[j]
        return pl.multiple_of(lax.rem(z // 2 + ahead, COLS) * 128, 128)

    loads = [
        pltpu.make_async_copy(
            table_hbm.at[:, pl.ds(col(j), 128)], tab.at[j], tab_sem.at[j])
        for j in range(COLS)
    ]
    for c in loads:
        c.start()
    for c in ins[1:]:
        c.start()

    barrier = pltpu.get_barrier_semaphore()
    for r in (1, NZ - 1):
        pl.semaphore_signal(barrier, inc=1, device_id=zpeer(r), device_id_type=MESH)
    for r in range(1, NX):
        pl.semaphore_signal(barrier, inc=1, device_id=xpeer(r), device_id_type=MESH)
    for r in range(1, NY):
        pl.semaphore_signal(barrier, inc=1, device_id=ypeer(r), device_id_type=MESH)

    def greet(k):
        for r in (1, NZ - 1):
            pl.semaphore_signal(hello.at[k], inc=1, device_id=zpeer(r), device_id_type=MESH)

    def greeted(k):
        pl.semaphore_wait(hello.at[k], 2)

    for c in ins[1:]:
        c.wait()
    for j in range(COLS):
        lanes = slice(j * 128, (j + 1) * 128)
        blob[0, j * K:(j + 1) * K, :] = grad_v[:, lanes].astype(F32)
        blob[0, 64 + 2 * j:65 + 2 * j, :] = hess_v[j:j + 1, :].astype(F32)
        blob[0, 65 + 2 * j:66 + 2 * j, :] = node_v[:, lanes].astype(F32)

    ins[0].wait()
    hot = jnp.where(iota((TAB, S), 0) == rows_v[...], 1.0, 0.0).astype(BF16)

    def ch_copy(src_slot, dst_slot, where, k):
        return pltpu.make_async_remote_copy(
            src_ref=blob.at[src_slot], dst_ref=blob.at[dst_slot],
            send_sem=ch_send.at[k], recv_sem=ch_recv.at[dst_slot],
            device_id=where, device_id_type=MESH,
        )

    first = [ch_copy(0, 4 - m, xpeer(2 * m), m) for m in range(1, 4)] + [ch_copy(0, 4, sibling, 0)]

    def chunk_z(i):
        return lax.rem(z + NZ + choose(i, (4, -3 * turn, 3 * turn, 2 * turn, -2 * turn, -turn, turn, 0)), NZ)

    def x_copy(i, m, other):
        peer_x = lax.rem(xd + 2 * m + NX, NX)
        peer_x = jnp.where(other, peer_x + sib_rel, peer_x) if other else peer_x
        row = pl.multiple_of(chunk_z(i) * (NX * OWN) + peer_x * OWN, OWN)
        if m == 0:
            send, recv, slot = sib_send, sib_recv, 0
        else:
            send, recv, slot = rx_send.at[i], rx_recv.at[i], (3 if other else 0) + 4 - m
        return pltpu.make_async_remote_copy(
            src_ref=pk.at[pl.ds(row, OWN), :],
            dst_ref=rx.at[slot, i],
            send_sem=send, recv_sem=recv,
            device_id=(z * NX + peer_x, y), device_id_type=MESH,
        )

    def start_chunk(i):
        for m in (2, 1, 3):
            x_copy(i, m, False).start()
            x_copy(i, m, True).start()

    for j in range(COLS):
        loads[j].wait()
        part = tab[j].astype(F32).astype(BF16)
        pk[pl.ds(col(j), 128), :] = lax.dot_general(
            part, hot, (((0,), (0,)), ((), ())), preferred_element_type=F32)
        if j == 0:
            pl.semaphore_wait(barrier, NX + NY)
            for c in first:
                c.start()
        for i in (2 * j, 2 * j + 1):
            if i < 2:
                start_chunk(i)
            x_copy(i, 0, True).start()
        if j == 0:
            greet(0)
        if j == 2:
            greeted(0)
            greet(1)

    def weights(slot, place):
        for j in range(COLS):
            g = blob[slot, j * K:(j + 1) * K, :]
            h = blob[slot, 64 + 2 * j:65 + 2 * j, :]
            n = blob[slot, 65 + 2 * j:66 + 2 * j, :]
            at0 = n == 0.0
            at1 = n == 1.0
            rest = jnp.where(iota((16, 128), 0) == 0, jnp.where(at0, h, 0.0),
                             jnp.where(iota((16, 128), 0) == 1, jnp.where(at1, h, 0.0), 0.0))
            full = jnp.concatenate(
                [jnp.where(at0, g, 0.0), jnp.where(at1, g, 0.0), rest], axis=0)
            wt[place, :, j * 128:(j + 1) * 128] = full.astype(BF16)

    level = iota((BINS, S), 0).astype(F32).astype(BF16)
    one = jnp.ones((), BF16)
    zero = jnp.zeros((), BF16)

    def below(value):
        return jnp.where(jnp.broadcast_to(value.astype(BF16), (BINS, S)) <= level, one, zero)

    def product(place, values):
        return nt(wt[place], jnp.concatenate([below(v) for v in values], axis=0))

    weights(0, 0)

    def own_chunk(i, carry):
        mine = chunk_z(i) * (NX * OWN) + xd * OWN
        acc[i] = product(0, [pk[pl.ds(mine + f, 1), :] for f in range(OWN)])
        return carry

    lax.fori_loop(0, NZ, own_chunk, 0)

    greeted(1)
    greet(2)

    sides = []
    for n in range(NODES):
        at = sf[n] - y * WIDTH
        inside = jnp.where((at >= 0) & (at < WIDTH), 1.0, 0.0).astype(F32)
        row = pk[pl.ds(jnp.clip(at, 0, WIDTH - 1), 1), :]
        sides.append(jnp.where(row <= sb[n].astype(F32), inside, 0.0))
    ind = jnp.concatenate([
        jnp.where(node_v[...] == 0, sides[0], sides[1]),
        jnp.full((1, S), jnp.where(y == 0, 1.0, 0.0).astype(F32)),
        jnp.zeros((14, S), F32)], axis=0).astype(BF16)
    part = nt(ind, wt[0])
    gap = jnp.zeros((1, 64 - WROWS), F32)
    lf[0] = jnp.concatenate([part[:1], gap, part[1:2], gap], axis=1)

    def l_copy(stage, dst, where):
        return pltpu.make_async_remote_copy(
            src_ref=lf.at[stage], dst_ref=dst, send_sem=l_send.at[stage], recv_sem=l_recv.at[stage],
            device_id=where, device_id_type=MESH)

    for r in range(1, NY):
        l_copy(0, lfy.at[NY - r - 1], ypeer(r)).start()

    second = [ch_copy(m, 4 + m, sibling, 3 + m) for m in range(1, 4)]
    for m in (3, 1, 2):
        first[3 - m].wait_recv()
        second[m - 1].start()
    for i in range(2,4):
        start_chunk(i)

    first[3].wait_recv()
    weights(4, 4)
    pltpu.make_async_copy(rx.at[0], rx.at[0], sib_recv).wait()

    def sib_chunk(i, carry):
        acc[i] += product(4, [rx[0, i, f:f + 1, :] for f in range(OWN)])
        return carry

    lax.fori_loop(0, NZ, sib_chunk, 0)

    for m in range(1, 4):
        weights(m, m)
    for c in second:
        c.wait_recv()
    for m in range(5, 8):
        weights(m, m)
    greeted(2)

    def z_copy(i):
        dz = choose(i, (-turn, -turn, turn, 2 * turn, -2 * turn, -turn, turn))
        return pltpu.make_async_remote_copy(
            src_ref=zs.at[i], dst_ref=rz.at[i],
            send_sem=rz_send.at[i], recv_sem=rz_recv.at[i],
            device_id=(lax.rem(z + NZ + dz, NZ) * NX + xd, y), device_id_type=MESH,
        )

    def chunk(i, carry):
        @pl.when(i + AHEAD < NZ)
        def _():
            start_chunk(i + AHEAD)

        six = rx.at[pl.ds(1, 6), 0]
        pltpu.make_async_copy(six, six, rx_recv.at[i]).wait()
        total = acc[i]
        for slot in range(1, 7):
            place = slot if slot < 4 else slot + 1
            total = total + product(place, [rx[slot, i, f:f + 1, :] for f in range(OWN)])
        for j in range(COLS):
            lanes = slice(j * 128, (j + 1) * 128)
            zs[i, j * 32:(j + 1) * 32, :] = total[:32, lanes]
            zs[i, 128 + 2 * j:130 + 2 * j, :] = total[32:34, lanes]

        @pl.when((i < 2) | (i == 5) | (i == 6))
        def _():
            z_copy(i).start()

        @pl.when((i == 3) | (i == 4) | (i == 6))
        def _():
            c = jnp.where(i == 6, 4, i - 1)
            pltpu.make_async_copy(rz.at[c - 2], rz.at[c - 2], rz_recv.at[c - 2]).wait()
            zs[c] = zs[c] + rz[c - 2]
            z_copy(c).start()

        @pl.when(i == 1)
        def _():
            pltpu.make_async_copy(lfy, lfy, l_recv.at[0]).wait()
            lf[1] = lf[0] + lfy[0] + lfy[1] + lfy[2]
            for r in range(1, NX):
                l_copy(1, lfx.at[NX - r - 1], xpeer(r)).start()

        @pl.when(i == 4)
        def _():
            pltpu.make_async_copy(lfx, lfx, l_recv.at[1]).wait()
            s = lf[1]
            for r in range(NX - 1):
                s = s + lfx[r]
            lf[2] = s
            for r in range(1, NZ):
                l_copy(2, lfz.at[NZ - r - 1], zpeer(r)).start()

        return carry

    lax.fori_loop(0, NZ, chunk, 0)
    pltpu.make_async_copy(lfz, lfz, l_recv.at[2]).wait()
    for i in (3, 4, 5, 6):
        pltpu.make_async_copy(rz.at[i], rz.at[i], rz_recv.at[i]).wait()
    left = zs[7] + rz[3] + rz[4] + rz[5] + rz[6]

    tot_g = jnp.broadcast_to(left[:32, BINS - 1:BINS], (32, 128))
    tot_h = jnp.broadcast_to(left[128:130, BINS - 1:BINS], (2, 128))

    def score(g, h):
        return jnp.sum(g * g, axis=0, keepdims=True) / (h + LAMBDA_REG)

    gains = []
    for j in range(COLS):
        for n in range(NODES):
            gl = left[j * 32 + n * K:j * 32 + (n + 1) * K]
            hl = left[128 + 2 * j + n:129 + 2 * j + n]
            gt = tot_g[n * K:(n + 1) * K]
            ht = tot_h[n:n + 1]
            gains.append(score(gl, hl) + score(gt - gl, ht - hl) - score(gt, ht))
    gains = jnp.concatenate(gains, axis=0) * (GAIN_WEIGHT / K)
    lane = iota((8, 128), 1)
    row8 = iota((8, 128), 0)
    low = jnp.max(jnp.where(lane < BINS, gains, -jnp.inf), axis=1, keepdims=True)
    high = jnp.max(jnp.where(lane >= BINS, gains, -jnp.inf), axis=1, keepdims=True)
    home = lax.rem(row8 + z, 2) * 64 + xd * OWN + (row8 // 2) * 2
    mine = jnp.where(lane == home, low, jnp.where(lane == home + 1, high, 0.0))
    mine = jnp.sum(mine, axis=0, keepdims=True)
    fin_own[...] = mine
    keep = pltpu.make_async_copy(fin_own, fin.at[d], out_sem.at[0])
    keep.start()

    def f_copy(to_z, r):
        return pltpu.make_async_remote_copy(
            src_ref=fin_own, dst_ref=fin.at[d], send_sem=f_send, recv_sem=f_recv,
            device_id=(to_z * NX + lax.rem(xd + r, NX), y), device_id_type=MESH)

    for to_z in range(NZ):
        for r in FAR[:-1]:
            f_copy(to_z, r).start()

        @pl.when(z != to_z)
        def _():
            f_copy(to_z, 0).start()

    s = lf[2]
    for r in range(NZ - 1):
        s = s + lfz[r]
    leaf_v[...] = s
    keep_leaf = pltpu.make_async_copy(leaf_v, leaf_sum, out_sem.at[1])
    keep_leaf.start()

    for c in first + second:
        c.wait_send()
    six = rx.at[pl.ds(1, 6), 0]
    for i in range(NZ):
        pltpu.make_async_copy(six, six, rx_send.at[i]).wait()
    pltpu.make_async_copy(rx.at[0], rx.at[0], sib_send).wait()
    for i in range(NZ - 1):
        pltpu.make_async_copy(rz.at[i], rz.at[i], rz_send.at[i]).wait()
    pltpu.make_async_copy(lfy, lfy, l_send.at[0]).wait()
    pltpu.make_async_copy(lfx, lfx, l_send.at[1]).wait()
    pltpu.make_async_copy(lfz, lfz, l_send.at[2]).wait()

    others = fin.at[pl.ds(0, NX * NZ - 1)]
    pltpu.make_async_copy(others, others, f_recv).wait()
    pltpu.make_async_copy(others, others, f_send).wait()
    keep.wait()
    keep_leaf.wait()


def assemble(fin, leaf_sum, best_ref, leaf_ref):
    lane = iota((1, 128), 1)
    for j in range(COLS):
        pair = []
        for q in (2 * j, 2 * j + 1):
            v = fin[q * NX]
            for r in range(1, NX):
                v = v + fin[q * NX + r]
            pair.append(v)
        best_ref[0:1, j * 128:(j + 1) * 128] = jnp.where(lane < 64, pair[0], pair[1])
        best_ref[1:2, j * 128:(j + 1) * 128] = pltpu.roll(
            jnp.where(lane < 64, pair[1], pair[0]), 64, axis=1)
    s = leaf_sum[...]
    tot = s[:, 64:128]
    lft = s[:, 0:64]
    for n in range(NODES):
        for side, part in enumerate((lft, tot - lft)):
            g = part[:, n * K:(n + 1) * K]
            h = part[:, 32 + n:33 + n]
            leaf_ref[2 * n + side:2 * n + side + 1, :] = -g / (h + LAMBDA_REG)


def shards(table, sample_rows, gradients, hessian, node_ids, split_feature, split_bin):
    vmem = pl.BlockSpec(memory_space=pltpu.VMEM)
    hbm = pl.BlockSpec(memory_space=pltpu.HBM)
    dma = pltpu.SemaphoreType.DMA
    row = pltpu.VMEM((1, 128), F32)
    fin, leaf_sum = pl.pallas_call(
        kernel,
        out_shape=(
            jax.ShapeDtypeStruct((NX * NZ, 1, 128), F32),
            jax.ShapeDtypeStruct((1, 128), F32),
        ),
        in_specs=[hbm] * 7,
        out_specs=(hbm, hbm),
        scratch_shapes=[
            pltpu.SMEM((NODES,), jnp.int32),
            pltpu.SMEM((NODES,), jnp.int32),
            pltpu.VMEM((COLS, TAB, 128), jnp.int32),
            pltpu.VMEM((1, S), jnp.int32),
            pltpu.VMEM((K, S), BF16),
            pltpu.VMEM((COLS, 128), BF16),
            pltpu.VMEM((1, S), jnp.int32),
            pltpu.VMEM((WIDTH, S), F32),
            pltpu.VMEM((NX - 1, NZ, OWN, S), F32),
            pltpu.VMEM((NX, 72, 128), F32),
            pltpu.VMEM((NX, WROWS, S), BF16),
            pltpu.VMEM((NZ, WROWS, OWN * BINS), F32),
            pltpu.VMEM((NZ, HROWS, 128), F32),
            pltpu.VMEM((NZ - 1, HROWS, 128), F32),
            pltpu.VMEM((3, 1, 128), F32),
            pltpu.VMEM((NY - 1, 1, 128), F32),
            pltpu.VMEM((NX - 1, 1, 128), F32),
            pltpu.VMEM((NZ - 1, 1, 128), F32),
            row,
            row,
            dma((6,)), dma((COLS,)),
            dma((NZ,)), dma((NZ,)),
            dma, dma,
            dma((7,)), dma((8,)),
            dma((NZ - 1,)), dma((NZ - 1,)),
            dma((3,)), dma((3,)),
            dma, dma,
            dma((2,)),
            pltpu.SemaphoreType.REGULAR((3,)),
        ],
        compiler_params=pltpu.CompilerParams(
            collective_id=0, has_side_effects=True, vmem_limit_bytes=60 * 2**20),
    )(
        split_feature, split_bin, table, sample_rows.reshape(1, S), gradients.T,
        hessian.reshape(COLS, 128), node_ids.reshape(1, S),
    )
    return pl.pallas_call(
        assemble,
        out_shape=(
            jax.ShapeDtypeStruct((NODES, WIDTH), F32),
            jax.ShapeDtypeStruct((2 * NODES, K), F32),
        ),
        in_specs=[vmem, vmem],
        out_specs=(vmem, vmem),
        compiler_params=pltpu.CompilerParams(vmem_limit_bytes=60 * 2**20),
    )(fin, leaf_sum)


def solution(mesh):
    return jax.shard_map(
        shards,
        mesh=mesh,
        in_specs=(P("dp", "feat"), P("dp"), P("dp", None), P("dp"), P("dp"), P(), P()),
        out_specs=(P(None, "feat"), P()),
        check_vma=False,
    )
```

```python
import jax
import jax.numpy as jnp
from jax import lax
from jax.experimental import pallas as pl
from jax.experimental.pallas import tpu as pltpu
from jax.sharding import PartitionSpec as P

BINS = 64
K = 16
NODES = 2
LAMBDA_REG = 1.0
GAIN_WEIGHT = 0.01

NX = 8
NZ = 8
NY = 4
S = 512
TAB = 1024
WIDTH = 512
OWN = 8
COLS = WIDTH // 128
WROWS = 48
HROWS = COLS * 32 + 8
AHEAD = 4
FAR = (4, 3, 5, 2, 6, 1, 7, 0)
MESH = pl.DeviceIdType.MESH
F32 = jnp.float32
BF16 = jnp.bfloat16


def iota(shape, dim):
    return lax.broadcasted_iota(jnp.int32, shape, dim)


def choose(i, values):
    out = values[-1]
    for k in range(len(values) - 2, -1, -1):
        out = jnp.where(i == k, values[k], out)
    return out


def nt(a, b):
    return lax.dot_general(a, b, (((1,), (1,)), ((), ())), preferred_element_type=F32)


def kernel(
    sf_hbm, sb_hbm, table_hbm, rows_hbm, grad_hbm, hess_hbm, node_hbm,
    fin, leaf_sum,
    sf, sb, tab, rows_v, grad_v, hess_v, node_v, pk, rx, blob, wt, acc, zs, rz,
    lf, lfy, lfx, lfz, lff, fin_own, leaf_v,
    in_sem, tab_sem, rx_send, rx_recv, sib_send, sib_recv, ch_send, ch_recv, rz_send, rz_recv,
    l_send, l_recv, f_send, f_recv, out_sem, hello,
):
    d = lax.axis_index("dp")
    y = lax.axis_index("feat")
    z = d // NX
    xd = d % NX
    core = xd % 2
    sib_rel = 1 - 2 * core
    turn = 1 - 2 * lax.rem(z, 2)

    def xpeer(r):
        return (z * NX + lax.rem(xd + r, NX), y)

    def zpeer(q):
        return (lax.rem(z + q, NZ) * NX + xd, y)

    def ypeer(r):
        return (d, lax.rem(y + r, NY))

    sibling = (d + sib_rel, y)

    ins = [
        pltpu.make_async_copy(src, dst, in_sem.at[k])
        for k, (src, dst) in enumerate((
            (rows_hbm, rows_v), (grad_hbm, grad_v), (hess_hbm, hess_v), (node_hbm, node_v),
            (sf_hbm, sf), (sb_hbm, sb)))
    ]
    ins[0].start()

    def col(j):
        ahead = (2, 2 - turn, 2 + turn, 0)[j]
        return pl.multiple_of(lax.rem(z // 2 + ahead, COLS) * 128, 128)

    loads = [
        pltpu.make_async_copy(
            table_hbm.at[:, pl.ds(col(j), 128)], tab.at[j], tab_sem.at[j])
        for j in range(COLS)
    ]
    for c in loads:
        c.start()
    for c in ins[1:]:
        c.start()

    barrier = pltpu.get_barrier_semaphore()
    for r in (1, NZ - 1):
        pl.semaphore_signal(barrier, inc=1, device_id=zpeer(r), device_id_type=MESH)
    for r in range(1, NX):
        pl.semaphore_signal(barrier, inc=1, device_id=xpeer(r), device_id_type=MESH)

    @pl.when(z == 0)
    def _():
        for r in range(1, NY):
            pl.semaphore_signal(barrier, inc=1, device_id=ypeer(r), device_id_type=MESH)

    def greet(k):
        for r in (1, NZ - 1):
            pl.semaphore_signal(hello.at[k], inc=1, device_id=zpeer(r), device_id_type=MESH)

    def greeted(k):
        pl.semaphore_wait(hello.at[k], 2)

    for c in ins[1:]:
        c.wait()
    for j in range(COLS):
        lanes = slice(j * 128, (j + 1) * 128)
        blob[0, j * K:(j + 1) * K, :] = grad_v[:, lanes].astype(F32)
        blob[0, 64 + 2 * j:65 + 2 * j, :] = hess_v[j:j + 1, :].astype(F32)
        blob[0, 65 + 2 * j:66 + 2 * j, :] = node_v[:, lanes].astype(F32)

    ins[0].wait()
    hot = jnp.where(iota((TAB, S), 0) == rows_v[...], 1.0, 0.0).astype(BF16)

    def ch_copy(src_slot, dst_slot, where, k):
        return pltpu.make_async_remote_copy(
            src_ref=blob.at[src_slot], dst_ref=blob.at[dst_slot],
            send_sem=ch_send.at[k], recv_sem=ch_recv.at[dst_slot],
            device_id=where, device_id_type=MESH,
        )

    first = [ch_copy(0, 4 - m, xpeer(2 * m), m) for m in range(1, 4)] + [ch_copy(0, 4, sibling, 0)]

    def chunk_z(i):
        return lax.rem(z + NZ + choose(i, (4, -3 * turn, 3 * turn, 2 * turn, -2 * turn, -turn, turn, 0)), NZ)

    def x_copy(i, m, other):
        peer_x = lax.rem(xd + 2 * m + NX, NX)
        peer_x = jnp.where(other, peer_x + sib_rel, peer_x) if other else peer_x
        row = pl.multiple_of(chunk_z(i) * (NX * OWN) + peer_x * OWN, OWN)
        if m == 0:
            send, recv, slot = sib_send, sib_recv, 0
        else:
            send, recv, slot = rx_send.at[i], rx_recv.at[i], (3 if other else 0) + 4 - m
        return pltpu.make_async_remote_copy(
            src_ref=pk.at[pl.ds(row, OWN), :],
            dst_ref=rx.at[slot, i],
            send_sem=send, recv_sem=recv,
            device_id=(z * NX + peer_x, y), device_id_type=MESH,
        )

    def start_chunk(i):
        for m in (2, 1, 3):
            x_copy(i, m, False).start()
            x_copy(i, m, True).start()

    for j in range(COLS):
        loads[j].wait()
        part = tab[j].astype(F32).astype(BF16)
        pk[pl.ds(col(j), 128), :] = lax.dot_general(
            part, hot, (((0,), (0,)), ((), ())), preferred_element_type=F32)
        if j == 0:
            pl.semaphore_wait(barrier, jnp.where(z == 0, NX + NY, NX + 1))
            for c in first:
                c.start()
        for i in (2 * j, 2 * j + 1):
            if i < 2:
                start_chunk(i)
            x_copy(i, 0, True).start()
        if j == 0:
            greet(0)
        if j == 2:
            greeted(0)
            greet(1)

    def weights(slot, place):
        for j in range(COLS):
            g = blob[slot, j * K:(j + 1) * K, :]
            h = blob[slot, 64 + 2 * j:65 + 2 * j, :]
            n = blob[slot, 65 + 2 * j:66 + 2 * j, :]
            at0 = n == 0.0
            at1 = n == 1.0
            rest = jnp.where(iota((16, 128), 0) == 0, jnp.where(at0, h, 0.0),
                             jnp.where(iota((16, 128), 0) == 1, jnp.where(at1, h, 0.0), 0.0))
            full = jnp.concatenate(
                [jnp.where(at0, g, 0.0), jnp.where(at1, g, 0.0), rest], axis=0)
            wt[place, :, j * 128:(j + 1) * 128] = full.astype(BF16)

    level = iota((BINS, S), 0).astype(F32).astype(BF16)
    one = jnp.ones((), BF16)
    zero = jnp.zeros((), BF16)

    def below(value):
        return jnp.where(jnp.broadcast_to(value.astype(BF16), (BINS, S)) <= level, one, zero)

    def product(place, values):
        return nt(wt[place], jnp.concatenate([below(v) for v in values], axis=0))

    weights(0, 0)

    def own_chunk(i, carry):
        mine = chunk_z(i) * (NX * OWN) + xd * OWN
        acc[i] = product(0, [pk[pl.ds(mine + f, 1), :] for f in range(OWN)])
        return carry

    lax.fori_loop(0, NZ, own_chunk, 0)

    greeted(1)
    greet(2)

    sides = []
    for n in range(NODES):
        at = sf[n] - y * WIDTH
        inside = jnp.where((at >= 0) & (at < WIDTH), 1.0, 0.0).astype(F32)
        row = pk[pl.ds(jnp.clip(at, 0, WIDTH - 1), 1), :]
        sides.append(jnp.where(row <= sb[n].astype(F32), inside, 0.0))
    ind = jnp.concatenate([
        jnp.where(node_v[...] == 0, sides[0], sides[1]),
        jnp.full((1, S), jnp.where(y == 0, 1.0, 0.0).astype(F32)),
        jnp.zeros((14, S), F32)], axis=0).astype(BF16)
    part = nt(ind, wt[0])
    gap = jnp.zeros((1, 64 - WROWS), F32)
    lf[0] = jnp.concatenate([part[:1], gap, part[1:2], gap], axis=1)

    def l_copy(stage, dst, where):
        return pltpu.make_async_remote_copy(
            src_ref=lf.at[stage], dst_ref=dst, send_sem=l_send.at[stage], recv_sem=l_recv.at[stage],
            device_id=where, device_id_type=MESH)

    for r in range(1, NX):
        l_copy(0, lfx.at[NX - r - 1], xpeer(r)).start()

    second = [ch_copy(m, 4 + m, sibling, 3 + m) for m in range(1, 4)]
    for m in (3, 1, 2):
        first[3 - m].wait_recv()
        second[m - 1].start()
    for i in range(2,4):
        start_chunk(i)

    first[3].wait_recv()
    weights(4, 4)
    pltpu.make_async_copy(rx.at[0], rx.at[0], sib_recv).wait()

    def sib_chunk(i, carry):
        acc[i] += product(4, [rx[0, i, f:f + 1, :] for f in range(OWN)])
        return carry

    lax.fori_loop(0, NZ, sib_chunk, 0)

    for m in range(1, 4):
        weights(m, m)
    for c in second:
        c.wait_recv()
    for m in range(5, 8):
        weights(m, m)
    greeted(2)

    def z_copy(i):
        dz = choose(i, (-turn, -turn, turn, 2 * turn, -2 * turn, -turn, turn))
        return pltpu.make_async_remote_copy(
            src_ref=zs.at[i], dst_ref=rz.at[i],
            send_sem=rz_send.at[i], recv_sem=rz_recv.at[i],
            device_id=(lax.rem(z + NZ + dz, NZ) * NX + xd, y), device_id_type=MESH,
        )

    def chunk(i, carry):
        @pl.when(i + AHEAD < NZ)
        def _():
            start_chunk(i + AHEAD)

        six = rx.at[pl.ds(1, 6), 0]
        pltpu.make_async_copy(six, six, rx_recv.at[i]).wait()
        total = acc[i]
        for slot in range(1, 7):
            place = slot if slot < 4 else slot + 1
            total = total + product(place, [rx[slot, i, f:f + 1, :] for f in range(OWN)])
        for j in range(COLS):
            lanes = slice(j * 128, (j + 1) * 128)
            zs[i, j * 32:(j + 1) * 32, :] = total[:32, lanes]
            zs[i, 128 + 2 * j:130 + 2 * j, :] = total[32:34, lanes]

        @pl.when((i < 2) | (i == 5) | (i == 6))
        def _():
            z_copy(i).start()

        @pl.when((i == 3) | (i == 4) | (i == 6))
        def _():
            c = jnp.where(i == 6, 4, i - 1)
            pltpu.make_async_copy(rz.at[c - 2], rz.at[c - 2], rz_recv.at[c - 2]).wait()
            zs[c] = zs[c] + rz[c - 2]
            z_copy(c).start()

        @pl.when(i == 1)
        def _():
            pltpu.make_async_copy(lfx, lfx, l_recv.at[0]).wait()
            s = lf[0]
            for r in range(NX - 1):
                s = s + lfx[r]
            lf[1] = s

        @pl.when((i == 1) & (z != 0))
        def _():
            l_copy(1, lfz.at[z - 1], (xd, y)).start()

        @pl.when((i == 6) & (z == 0))
        def _():
            pltpu.make_async_copy(lfz, lfz, l_recv.at[1]).wait()
            s = lf[1]
            for r in range(NZ - 1):
                s = s + lfz[r]
            lf[2] = s
            for r in range(1, NY):
                l_copy(2, lfy.at[NY - r - 1], ypeer(r)).start()

        return carry

    lax.fori_loop(0, NZ, chunk, 0)
    for i in (3, 4, 5, 6):
        pltpu.make_async_copy(rz.at[i], rz.at[i], rz_recv.at[i]).wait()
    left = zs[7] + rz[3] + rz[4] + rz[5] + rz[6]

    tot_g = jnp.broadcast_to(left[:32, BINS - 1:BINS], (32, 128))
    tot_h = jnp.broadcast_to(left[128:130, BINS - 1:BINS], (2, 128))

    def score(g, h):
        return jnp.sum(g * g, axis=0, keepdims=True) / (h + LAMBDA_REG)

    gains = []
    for j in range(COLS):
        for n in range(NODES):
            gl = left[j * 32 + n * K:j * 32 + (n + 1) * K]
            hl = left[128 + 2 * j + n:129 + 2 * j + n]
            gt = tot_g[n * K:(n + 1) * K]
            ht = tot_h[n:n + 1]
            gains.append(score(gl, hl) + score(gt - gl, ht - hl) - score(gt, ht))
    gains = jnp.concatenate(gains, axis=0) * (GAIN_WEIGHT / K)
    lane = iota((8, 128), 1)
    row8 = iota((8, 128), 0)
    low = jnp.max(jnp.where(lane < BINS, gains, -jnp.inf), axis=1, keepdims=True)
    high = jnp.max(jnp.where(lane >= BINS, gains, -jnp.inf), axis=1, keepdims=True)
    home = lax.rem(row8 + z, 2) * 64 + xd * OWN + (row8 // 2) * 2
    mine = jnp.where(lane == home, low, jnp.where(lane == home + 1, high, 0.0))
    mine = jnp.sum(mine, axis=0, keepdims=True)
    fin_own[...] = mine
    keep = pltpu.make_async_copy(fin_own, fin.at[d], out_sem.at[0])
    keep.start()

    def f_copy(to_z, r):
        return pltpu.make_async_remote_copy(
            src_ref=fin_own, dst_ref=fin.at[d], send_sem=f_send, recv_sem=f_recv,
            device_id=(to_z * NX + lax.rem(xd + r, NX), y), device_id_type=MESH)

    for to_z in range(NZ):
        for r in FAR[:-1]:
            f_copy(to_z, r).start()

        @pl.when(z != to_z)
        def _():
            f_copy(to_z, 0).start()

    @pl.when(z == 0)
    def _():
        pltpu.make_async_copy(lfy, lfy, l_recv.at[2]).wait()
        s = lf[2] + lfy[0] + lfy[1] + lfy[2]
        lf[3] = s
        for r in FAR[:-1]:
            l_copy(3, lff, zpeer(r)).start()
        leaf_v[...] = s

    @pl.when(z != 0)
    def _():
        pltpu.make_async_copy(lff, lff, l_recv.at[3]).wait()
        leaf_v[...] = lff[...]

    keep_leaf = pltpu.make_async_copy(leaf_v, leaf_sum, out_sem.at[1])
    keep_leaf.start()

    for c in first + second:
        c.wait_send()
    six = rx.at[pl.ds(1, 6), 0]
    for i in range(NZ):
        pltpu.make_async_copy(six, six, rx_send.at[i]).wait()
    pltpu.make_async_copy(rx.at[0], rx.at[0], sib_send).wait()
    for i in range(NZ - 1):
        pltpu.make_async_copy(rz.at[i], rz.at[i], rz_send.at[i]).wait()
    pltpu.make_async_copy(lfx, lfx, l_send.at[0]).wait()

    @pl.when(z != 0)
    def _():
        pltpu.make_async_copy(lff, lff, l_send.at[1]).wait()

    @pl.when(z == 0)
    def _():
        pltpu.make_async_copy(lfy, lfy, l_send.at[2]).wait()
        pltpu.make_async_copy(lfz, lfz, l_send.at[3]).wait()

    others = fin.at[pl.ds(0, NX * NZ - 1)]
    pltpu.make_async_copy(others, others, f_recv).wait()
    pltpu.make_async_copy(others, others, f_send).wait()
    keep.wait()
    keep_leaf.wait()


def assemble(fin, leaf_sum, best_ref, leaf_ref):
    lane = iota((1, 128), 1)
    for j in range(COLS):
        pair = []
        for q in (2 * j, 2 * j + 1):
            v = fin[q * NX]
            for r in range(1, NX):
                v = v + fin[q * NX + r]
            pair.append(v)
        best_ref[0:1, j * 128:(j + 1) * 128] = jnp.where(lane < 64, pair[0], pair[1])
        best_ref[1:2, j * 128:(j + 1) * 128] = pltpu.roll(
            jnp.where(lane < 64, pair[1], pair[0]), 64, axis=1)
    s = leaf_sum[...]
    tot = s[:, 64:128]
    lft = s[:, 0:64]
    for n in range(NODES):
        for side, part in enumerate((lft, tot - lft)):
            g = part[:, n * K:(n + 1) * K]
            h = part[:, 32 + n:33 + n]
            leaf_ref[2 * n + side:2 * n + side + 1, :] = -g / (h + LAMBDA_REG)


def shards(table, sample_rows, gradients, hessian, node_ids, split_feature, split_bin):
    vmem = pl.BlockSpec(memory_space=pltpu.VMEM)
    hbm = pl.BlockSpec(memory_space=pltpu.HBM)
    dma = pltpu.SemaphoreType.DMA
    row = pltpu.VMEM((1, 128), F32)
    fin, leaf_sum = pl.pallas_call(
        kernel,
        out_shape=(
            jax.ShapeDtypeStruct((NX * NZ, 1, 128), F32),
            jax.ShapeDtypeStruct((1, 128), F32),
        ),
        in_specs=[hbm] * 7,
        out_specs=(hbm, hbm),
        scratch_shapes=[
            pltpu.SMEM((NODES,), jnp.int32),
            pltpu.SMEM((NODES,), jnp.int32),
            pltpu.VMEM((COLS, TAB, 128), jnp.int32),
            pltpu.VMEM((1, S), jnp.int32),
            pltpu.VMEM((K, S), BF16),
            pltpu.VMEM((COLS, 128), BF16),
            pltpu.VMEM((1, S), jnp.int32),
            pltpu.VMEM((WIDTH, S), F32),
            pltpu.VMEM((NX - 1, NZ, OWN, S), F32),
            pltpu.VMEM((NX, 72, 128), F32),
            pltpu.VMEM((NX, WROWS, S), BF16),
            pltpu.VMEM((NZ, WROWS, OWN * BINS), F32),
            pltpu.VMEM((NZ, HROWS, 128), F32),
            pltpu.VMEM((NZ - 1, HROWS, 128), F32),
            pltpu.VMEM((4, 1, 128), F32),
            pltpu.VMEM((NY - 1, 1, 128), F32),
            pltpu.VMEM((NX - 1, 1, 128), F32),
            pltpu.VMEM((NZ - 1, 1, 128), F32),
            row,
            row,
            row,
            dma((6,)), dma((COLS,)),
            dma((NZ,)), dma((NZ,)),
            dma, dma,
            dma((7,)), dma((8,)),
            dma((NZ - 1,)), dma((NZ - 1,)),
            dma((4,)), dma((4,)),
            dma, dma,
            dma((2,)),
            pltpu.SemaphoreType.REGULAR((3,)),
        ],
        compiler_params=pltpu.CompilerParams(
            collective_id=0, has_side_effects=True, vmem_limit_bytes=60 * 2**20),
    )(
        split_feature, split_bin, table, sample_rows.reshape(1, S), gradients.T,
        hessian.reshape(COLS, 128), node_ids.reshape(1, S),
    )
    return pl.pallas_call(
        assemble,
        out_shape=(
            jax.ShapeDtypeStruct((NODES, WIDTH), F32),
            jax.ShapeDtypeStruct((2 * NODES, K), F32),
        ),
        in_specs=[vmem, vmem],
        out_specs=(vmem, vmem),
        compiler_params=pltpu.CompilerParams(vmem_limit_bytes=60 * 2**20),
    )(fin, leaf_sum)


def solution(mesh):
    return jax.shard_map(
        shards,
        mesh=mesh,
        in_specs=(P("dp", "feat"), P("dp"), P("dp", None), P("dp"), P("dp"), P(), P()),
        out_specs=(P(None, "feat"), P()),
        check_vma=False,
    )
```

```python
import jax
import jax.numpy as jnp
from jax import lax
from jax.experimental import pallas as pl
from jax.experimental.pallas import tpu as pltpu
from jax.sharding import PartitionSpec as P

BINS = 64
K = 16
NODES = 2
LAMBDA_REG = 1.0
GAIN_WEIGHT = 0.01

NX = 8
NZ = 8
NY = 4
S = 512
TAB = 1024
WIDTH = 512
OWN = 8
COLS = WIDTH // 128
WROWS = 48
HROWS = COLS * 32 + 8
AHEAD = 4
FAR = (4, 3, 5, 2, 6, 1, 7, 0)
MESH = pl.DeviceIdType.MESH
F32 = jnp.float32
BF16 = jnp.bfloat16


def iota(shape, dim):
    return lax.broadcasted_iota(jnp.int32, shape, dim)


def choose(i, values):
    out = values[-1]
    for k in range(len(values) - 2, -1, -1):
        out = jnp.where(i == k, values[k], out)
    return out


def nt(a, b):
    return lax.dot_general(a, b, (((1,), (1,)), ((), ())), preferred_element_type=F32)


def kernel(
    sf_hbm, sb_hbm, table_hbm, rows_hbm, grad_hbm, hess_hbm, node_hbm,
    fin, leaf_sum,
    sf, sb, tab, rows_v, grad_v, hess_v, node_v, pk, rx, blob, wt, acc, zs, rz,
    lf, lfy, lfx, lfz, lff, fin_own, leaf_v,
    in_sem, tab_sem, rx_send, rx_recv, sib_send, sib_recv, ch_send, ch_recv, rz_send, rz_recv,
    l_send, l_recv, f_send, f_recv, out_sem, hello,
):
    d = lax.axis_index("dp")
    y = lax.axis_index("feat")
    z = d // NX
    xd = d % NX
    core = xd % 2
    sib_rel = 1 - 2 * core
    turn = 1 - 2 * lax.rem(z, 2)

    def xpeer(r):
        return (z * NX + lax.rem(xd + r, NX), y)

    def zpeer(q):
        return (lax.rem(z + q, NZ) * NX + xd, y)

    def ypeer(r):
        return (d, lax.rem(y + r, NY))

    sibling = (d + sib_rel, y)

    ins = [
        pltpu.make_async_copy(src, dst, in_sem.at[k])
        for k, (src, dst) in enumerate((
            (rows_hbm, rows_v), (grad_hbm, grad_v), (hess_hbm, hess_v), (node_hbm, node_v),
            (sf_hbm, sf), (sb_hbm, sb)))
    ]
    ins[0].start()

    def col(j):
        ahead = (2, 2 - turn, 2 + turn, 0)[j]
        return pl.multiple_of(lax.rem(z // 2 + ahead, COLS) * 128, 128)

    loads = [
        pltpu.make_async_copy(
            table_hbm.at[:, pl.ds(col(j), 128)], tab.at[j], tab_sem.at[j])
        for j in range(COLS)
    ]
    for c in loads:
        c.start()
    for c in ins[1:]:
        c.start()

    barrier = pltpu.get_barrier_semaphore()
    for r in (1, NZ - 1):
        pl.semaphore_signal(barrier, inc=1, device_id=zpeer(r), device_id_type=MESH)
    for r in range(1, NX):
        pl.semaphore_signal(barrier, inc=1, device_id=xpeer(r), device_id_type=MESH)

    @pl.when(z == 0)
    def _():
        for r in range(1, NY):
            pl.semaphore_signal(barrier, inc=1, device_id=ypeer(r), device_id_type=MESH)

    def greet(k):
        for r in (1, NZ - 1):
            pl.semaphore_signal(hello.at[k], inc=1, device_id=zpeer(r), device_id_type=MESH)

    def greeted(k):
        pl.semaphore_wait(hello.at[k], 2)

    for c in ins[1:]:
        c.wait()
    for j in range(COLS):
        lanes = slice(j * 128, (j + 1) * 128)
        blob[0, j * K:(j + 1) * K, :] = grad_v[:, lanes].astype(F32)
        blob[0, 64 + 2 * j:65 + 2 * j, :] = hess_v[j:j + 1, :].astype(F32)
        blob[0, 65 + 2 * j:66 + 2 * j, :] = node_v[:, lanes].astype(F32)

    ins[0].wait()
    hot = jnp.where(iota((TAB, S), 0) == rows_v[...], 1.0, 0.0).astype(BF16)

    def ch_copy(src_slot, dst_slot, where, k):
        return pltpu.make_async_remote_copy(
            src_ref=blob.at[src_slot], dst_ref=blob.at[dst_slot],
            send_sem=ch_send.at[k], recv_sem=ch_recv.at[dst_slot],
            device_id=where, device_id_type=MESH,
        )

    first = [ch_copy(0, 4 - m, xpeer(2 * m), m) for m in range(1, 4)] + [ch_copy(0, 4, sibling, 0)]

    def chunk_z(i):
        return lax.rem(z + NZ + choose(i, (4, -3 * turn, 3 * turn, 2 * turn, -2 * turn, -turn, turn, 0)), NZ)

    def x_copy(i, m, other):
        peer_x = lax.rem(xd + 2 * m + NX, NX)
        peer_x = jnp.where(other, peer_x + sib_rel, peer_x) if other else peer_x
        row = pl.multiple_of(chunk_z(i) * (NX * OWN) + peer_x * OWN, OWN)
        if m == 0:
            send, recv, slot = sib_send, sib_recv, 0
        else:
            send, recv, slot = rx_send.at[i], rx_recv.at[i], (3 if other else 0) + 4 - m
        return pltpu.make_async_remote_copy(
            src_ref=pk.at[pl.ds(row, OWN), :],
            dst_ref=rx.at[slot, i],
            send_sem=send, recv_sem=recv,
            device_id=(z * NX + peer_x, y), device_id_type=MESH,
        )

    def start_chunk(i):
        for m in (2, 1, 3):
            x_copy(i, m, False).start()
            x_copy(i, m, True).start()

    for j in range(COLS):
        loads[j].wait()
        part = tab[j].astype(F32).astype(BF16)
        pk[pl.ds(col(j), 128), :] = lax.dot_general(
            part, hot, (((0,), (0,)), ((), ())), preferred_element_type=F32)
        if j == 0:
            pl.semaphore_wait(barrier, jnp.where(z == 0, NX + NY, NX + 1))
            for c in first:
                c.start()
        for i in (2 * j, 2 * j + 1):
            if i < 2:
                start_chunk(i)
            x_copy(i, 0, True).start()
        if j == 0:
            greet(0)
        if j == 2:
            greeted(0)
            greet(1)

    def weights(slot, place):
        for j in range(COLS):
            g = blob[slot, j * K:(j + 1) * K, :]
            h = blob[slot, 64 + 2 * j:65 + 2 * j, :]
            n = blob[slot, 65 + 2 * j:66 + 2 * j, :]
            at0 = n == 0.0
            at1 = n == 1.0
            rest = jnp.where(iota((16, 128), 0) == 0, jnp.where(at0, h, 0.0),
                             jnp.where(iota((16, 128), 0) == 1, jnp.where(at1, h, 0.0), 0.0))
            full = jnp.concatenate(
                [jnp.where(at0, g, 0.0), jnp.where(at1, g, 0.0), rest], axis=0)
            wt[place, :, j * 128:(j + 1) * 128] = full.astype(BF16)

    level = iota((BINS, S), 0).astype(F32).astype(BF16)
    one = jnp.ones((), BF16)
    zero = jnp.zeros((), BF16)

    def below(value):
        return jnp.where(jnp.broadcast_to(value.astype(BF16), (BINS, S)) <= level, one, zero)

    def product(place, values):
        return nt(wt[place], jnp.concatenate([below(v) for v in values], axis=0))

    weights(0, 0)

    def own_chunk(i, carry):
        mine = chunk_z(i) * (NX * OWN) + xd * OWN
        acc[i] = product(0, [pk[pl.ds(mine + f, 1), :] for f in range(OWN)])
        return carry

    lax.fori_loop(0, NZ, own_chunk, 0)

    greeted(1)
    greet(2)

    sides = []
    for n in range(NODES):
        at = sf[n] - y * WIDTH
        inside = jnp.where((at >= 0) & (at < WIDTH), 1.0, 0.0).astype(F32)
        row = pk[pl.ds(jnp.clip(at, 0, WIDTH - 1), 1), :]
        sides.append(jnp.where(row <= sb[n].astype(F32), inside, 0.0))
    ind = jnp.concatenate([
        jnp.where(node_v[...] == 0, sides[0], sides[1]),
        jnp.full((1, S), jnp.where(y == 0, 1.0, 0.0).astype(F32)),
        jnp.zeros((14, S), F32)], axis=0).astype(BF16)
    part = nt(ind, wt[0])
    gap = jnp.zeros((1, 64 - WROWS), F32)
    lf[0] = jnp.concatenate([part[:1], gap, part[1:2], gap], axis=1)

    def l_copy(stage, dst, where):
        return pltpu.make_async_remote_copy(
            src_ref=lf.at[stage], dst_ref=dst, send_sem=l_send.at[stage], recv_sem=l_recv.at[stage],
            device_id=where, device_id_type=MESH)

    for r in range(1, NX):
        l_copy(0, lfx.at[NX - r - 1], xpeer(r)).start()

    second = [ch_copy(m, 4 + m, sibling, 3 + m) for m in range(1, 4)]
    for m in (3, 1, 2):
        first[3 - m].wait_recv()
        second[m - 1].start()
    for i in range(2,4):
        start_chunk(i)

    first[3].wait_recv()
    weights(4, 4)
    pltpu.make_async_copy(rx.at[0], rx.at[0], sib_recv).wait()

    def sib_chunk(i, carry):
        acc[i] += product(4, [rx[0, i, f:f + 1, :] for f in range(OWN)])
        return carry

    lax.fori_loop(0, NZ, sib_chunk, 0)

    for m in range(1, 4):
        weights(m, m)
    for c in second:
        c.wait_recv()
    for m in range(5, 8):
        weights(m, m)
    greeted(2)

    def z_copy(i):
        dz = choose(i, (-turn, -turn, turn, 2 * turn, -2 * turn, -turn, turn))
        return pltpu.make_async_remote_copy(
            src_ref=zs.at[i], dst_ref=rz.at[i],
            send_sem=rz_send.at[i], recv_sem=rz_recv.at[i],
            device_id=(lax.rem(z + NZ + dz, NZ) * NX + xd, y), device_id_type=MESH,
        )

    def chunk(i, carry):
        @pl.when(i + AHEAD < NZ)
        def _():
            start_chunk(i + AHEAD)

        six = rx.at[pl.ds(1, 6), 0]
        pltpu.make_async_copy(six, six, rx_recv.at[i]).wait()
        total = acc[i]
        for slot in range(1, 7):
            place = slot if slot < 4 else slot + 1
            total = total + product(place, [rx[slot, i, f:f + 1, :] for f in range(OWN)])
        for j in range(COLS):
            lanes = slice(j * 128, (j + 1) * 128)
            zs[i, j * 32:(j + 1) * 32, :] = total[:32, lanes]
            zs[i, 128 + 2 * j:130 + 2 * j, :] = total[32:34, lanes]

        @pl.when((i < 2) | (i == 5) | (i == 6))
        def _():
            z_copy(i).start()

        @pl.when((i == 3) | (i == 4) | (i == 6))
        def _():
            c = jnp.where(i == 6, 4, i - 1)
            pltpu.make_async_copy(rz.at[c - 2], rz.at[c - 2], rz_recv.at[c - 2]).wait()
            zs[c] = zs[c] + rz[c - 2]
            z_copy(c).start()

        @pl.when(i == 2)
        def _():
            pltpu.make_async_copy(lfx, lfx, l_recv.at[0]).wait()
            s = lf[0]
            for r in range(NX - 1):
                s = s + lfx[r]
            lf[1] = s

        @pl.when((i == 2) & (z != 0))
        def _():
            l_copy(1, lfz.at[z - 1], (xd, y)).start()

        @pl.when((i == 6) & (z == 0))
        def _():
            pltpu.make_async_copy(lfz, lfz, l_recv.at[1]).wait()
            s = lf[1]
            for r in range(NZ - 1):
                s = s + lfz[r]
            lf[2] = s
            for r in range(1, NY):
                l_copy(2, lfy.at[NY - r - 1], ypeer(r)).start()

        return carry

    lax.fori_loop(0, NZ, chunk, 0)
    for i in (3, 4, 5, 6):
        pltpu.make_async_copy(rz.at[i], rz.at[i], rz_recv.at[i]).wait()
    left = zs[7] + rz[3] + rz[4] + rz[5] + rz[6]

    tot_g = jnp.broadcast_to(left[:32, BINS - 1:BINS], (32, 128))
    tot_h = jnp.broadcast_to(left[128:130, BINS - 1:BINS], (2, 128))

    def score(g, h):
        return jnp.sum(g * g, axis=0, keepdims=True) / (h + LAMBDA_REG)

    gains = []
    for j in range(COLS):
        for n in range(NODES):
            gl = left[j * 32 + n * K:j * 32 + (n + 1) * K]
            hl = left[128 + 2 * j + n:129 + 2 * j + n]
            gt = tot_g[n * K:(n + 1) * K]
            ht = tot_h[n:n + 1]
            gains.append(score(gl, hl) + score(gt - gl, ht - hl) - score(gt, ht))
    gains = jnp.concatenate(gains, axis=0) * (GAIN_WEIGHT / K)
    lane = iota((8, 128), 1)
    row8 = iota((8, 128), 0)
    low = jnp.max(jnp.where(lane < BINS, gains, -jnp.inf), axis=1, keepdims=True)
    high = jnp.max(jnp.where(lane >= BINS, gains, -jnp.inf), axis=1, keepdims=True)
    home = lax.rem(row8 + z, 2) * 64 + xd * OWN + (row8 // 2) * 2
    mine = jnp.where(lane == home, low, jnp.where(lane == home + 1, high, 0.0))
    mine = jnp.sum(mine, axis=0, keepdims=True)
    fin_own[...] = mine
    keep = pltpu.make_async_copy(fin_own, fin.at[d], out_sem.at[0])
    keep.start()

    def f_copy(to_z, r):
        return pltpu.make_async_remote_copy(
            src_ref=fin_own, dst_ref=fin.at[d], send_sem=f_send, recv_sem=f_recv,
            device_id=(to_z * NX + lax.rem(xd + r, NX), y), device_id_type=MESH)

    for to_z in range(NZ):
        for r in FAR[:-1]:
            f_copy(to_z, r).start()

        @pl.when(z != to_z)
        def _():
            f_copy(to_z, 0).start()

    @pl.when(z == 0)
    def _():
        pltpu.make_async_copy(lfy, lfy, l_recv.at[2]).wait()
        s = lf[2] + lfy[0] + lfy[1] + lfy[2]
        lf[3] = s
        for r in FAR[:-1]:
            l_copy(3, lff, zpeer(r)).start()
        leaf_v[...] = s

    @pl.when(z != 0)
    def _():
        pltpu.make_async_copy(lff, lff, l_recv.at[3]).wait()
        leaf_v[...] = lff[...]

    keep_leaf = pltpu.make_async_copy(leaf_v, leaf_sum, out_sem.at[1])
    keep_leaf.start()

    for c in first + second:
        c.wait_send()
    six = rx.at[pl.ds(1, 6), 0]
    for i in range(NZ):
        pltpu.make_async_copy(six, six, rx_send.at[i]).wait()
    pltpu.make_async_copy(rx.at[0], rx.at[0], sib_send).wait()
    for i in range(NZ - 1):
        pltpu.make_async_copy(rz.at[i], rz.at[i], rz_send.at[i]).wait()
    pltpu.make_async_copy(lfx, lfx, l_send.at[0]).wait()

    @pl.when(z != 0)
    def _():
        pltpu.make_async_copy(lff, lff, l_send.at[1]).wait()

    @pl.when(z == 0)
    def _():
        pltpu.make_async_copy(lfy, lfy, l_send.at[2]).wait()
        pltpu.make_async_copy(lfz, lfz, l_send.at[3]).wait()

    others = fin.at[pl.ds(0, NX * NZ - 1)]
    pltpu.make_async_copy(others, others, f_recv).wait()
    pltpu.make_async_copy(others, others, f_send).wait()
    keep.wait()
    keep_leaf.wait()


def assemble(fin, leaf_sum, best_ref, leaf_ref):
    lane = iota((1, 128), 1)
    for j in range(COLS):
        pair = []
        for q in (2 * j, 2 * j + 1):
            v = fin[q * NX]
            for r in range(1, NX):
                v = v + fin[q * NX + r]
            pair.append(v)
        best_ref[0:1, j * 128:(j + 1) * 128] = jnp.where(lane < 64, pair[0], pair[1])
        best_ref[1:2, j * 128:(j + 1) * 128] = pltpu.roll(
            jnp.where(lane < 64, pair[1], pair[0]), 64, axis=1)
    s = leaf_sum[...]
    tot = s[:, 64:128]
    lft = s[:, 0:64]
    for n in range(NODES):
        for side, part in enumerate((lft, tot - lft)):
            g = part[:, n * K:(n + 1) * K]
            h = part[:, 32 + n:33 + n]
            leaf_ref[2 * n + side:2 * n + side + 1, :] = -g / (h + LAMBDA_REG)


def shards(table, sample_rows, gradients, hessian, node_ids, split_feature, split_bin):
    vmem = pl.BlockSpec(memory_space=pltpu.VMEM)
    hbm = pl.BlockSpec(memory_space=pltpu.HBM)
    dma = pltpu.SemaphoreType.DMA
    row = pltpu.VMEM((1, 128), F32)
    fin, leaf_sum = pl.pallas_call(
        kernel,
        out_shape=(
            jax.ShapeDtypeStruct((NX * NZ, 1, 128), F32),
            jax.ShapeDtypeStruct((1, 128), F32),
        ),
        in_specs=[hbm] * 7,
        out_specs=(hbm, hbm),
        scratch_shapes=[
            pltpu.SMEM((NODES,), jnp.int32),
            pltpu.SMEM((NODES,), jnp.int32),
            pltpu.VMEM((COLS, TAB, 128), jnp.int32),
            pltpu.VMEM((1, S), jnp.int32),
            pltpu.VMEM((K, S), BF16),
            pltpu.VMEM((COLS, 128), BF16),
            pltpu.VMEM((1, S), jnp.int32),
            pltpu.VMEM((WIDTH, S), F32),
            pltpu.VMEM((NX - 1, NZ, OWN, S), F32),
            pltpu.VMEM((NX, 72, 128), F32),
            pltpu.VMEM((NX, WROWS, S), BF16),
            pltpu.VMEM((NZ, WROWS, OWN * BINS), F32),
            pltpu.VMEM((NZ, HROWS, 128), F32),
            pltpu.VMEM((NZ - 1, HROWS, 128), F32),
            pltpu.VMEM((4, 1, 128), F32),
            pltpu.VMEM((NY - 1, 1, 128), F32),
            pltpu.VMEM((NX - 1, 1, 128), F32),
            pltpu.VMEM((NZ - 1, 1, 128), F32),
            row,
            row,
            row,
            dma((6,)), dma((COLS,)),
            dma((NZ,)), dma((NZ,)),
            dma, dma,
            dma((7,)), dma((8,)),
            dma((NZ - 1,)), dma((NZ - 1,)),
            dma((4,)), dma((4,)),
            dma, dma,
            dma((2,)),
            pltpu.SemaphoreType.REGULAR((3,)),
        ],
        compiler_params=pltpu.CompilerParams(
            collective_id=0, has_side_effects=True, vmem_limit_bytes=60 * 2**20),
    )(
        split_feature, split_bin, table, sample_rows.reshape(1, S), gradients.T,
        hessian.reshape(COLS, 128), node_ids.reshape(1, S),
    )
    return pl.pallas_call(
        assemble,
        out_shape=(
            jax.ShapeDtypeStruct((NODES, WIDTH), F32),
            jax.ShapeDtypeStruct((2 * NODES, K), F32),
        ),
        in_specs=[vmem, vmem],
        out_specs=(vmem, vmem),
        compiler_params=pltpu.CompilerParams(vmem_limit_bytes=60 * 2**20),
    )(fin, leaf_sum)


def solution(mesh):
    return jax.shard_map(
        shards,
        mesh=mesh,
        in_specs=(P("dp", "feat"), P("dp"), P("dp", None), P("dp"), P("dp"), P(), P()),
        out_specs=(P(None, "feat"), P()),
        check_vma=False,
    )
```
